1024 devices in a mesh: seq: 128 (over z, y), head: 8 (over x, core).
Axes of the slice: x: 4, y: 4, z: 32, core: 2. Of those that a mesh axis runs over, the one named last changes fastest.
Arguments:
- query: bfloat16 [8192, 2048], P('seq', 'head'), may hold values from -16 to 16
- key_states: bfloat16 [8192, 2048], P('seq', 'head'), may hold values from -16 to 16
- value_states: bfloat16 [8192, 2048], P('seq', 'head'), may hold values from -6 to 6
- doc_ids: int32 [8192], P('seq'), may hold values from 0 to 3, never falling along the last dimension, each value on 1 to 4096 neighbouring positions
- out_weight: bfloat16 [2048, 4096], P('head', 'seq'), may hold values from -0.5 to 0.5
- residual: bfloat16 [8192, 4096], P('seq', 'head'), may hold values from -6 to 6
Outputs:
- mixed: bfloat16 [8192, 4096], P('seq', 'head')
The draws below stay inside these ranges and needn't reach their ends.
Inputs may be any that keep to these rules, and one draw needn't show every extreme that they name: doc_ids never fall along the sequence; every document has 1 to 4096 positions, and one has exactly 4096.
All inputs are finite; a program needn't handle non-finite values.
Results may differ from the reference program's by a relative error of at most 0.0055.
Values may be sent and summed in bfloat16 or wider, within the bound.
No kernel may reach another device: no remote copies, remote signals or barrier semaphores. Data moves between devices by JAX's collectives and lax.ppermute only.
A program may use at most 64 MiB of HBM per device.

```python
import math
import jax
import jax.numpy as jnp
import numpy as np
from jax import lax

D = 4096
HEAD_DIM = 128
HEADS = 16
DOCS = 4
SEQ = 8192
DOC_MOST = 4096


def drawn_pair(key):
    base = jax.random.fold_in(key, 7)
    first, second = jax.random.split(base, 2)
    width = HEADS * HEAD_DIM
    queries = 1.7 * jnp.clip(jax.random.normal(first, (SEQ, width), jnp.float32), -4.5, 4.5)
    keys = 1.7 * jnp.clip(jax.random.normal(second, (SEQ, width), jnp.float32), -4.5, 4.5)
    return (queries, keys)


def draw_query(key, part):
    return drawn_pair(key)[0].astype(jnp.bfloat16)


def draw_key_states(key, part):
    return drawn_pair(key)[1].astype(jnp.bfloat16)


def spiked(drawn, rng, source, target, blocks, factor):
    owner, partner = [(jnp.arange(drawn.shape[position]) // (drawn.shape[position] // blocks)).reshape([-1 if axis == position else 1 for axis in range(drawn.ndim)]) for position in (source, target)]
    chosen = jax.random.permutation(rng, blocks)[partner]
    strong = (owner == chosen) | (owner == (partner + blocks // 2) % blocks)
    return jnp.where(strong, factor * drawn, drawn)


def block_scale(own_key, dims, cuts, least, largest):
    def one(dim, parts):
        heights = jax.random.uniform(jax.random.fold_in(jax.random.fold_in(own_key, 6), dim), (parts,), jnp.float32, least / len(cuts), largest / len(cuts))
        return jnp.repeat(jnp.exp(heights), dims[dim] // parts).reshape((-1,) + (1,) * (len(dims) - dim - 1))

    level = one(*cuts[0])
    for cut in cuts[1:]:
        level = level * one(*cut)
    return level


def split_up(count, total, most, skew):
    portions = [(1 << 20) // math.isqrt(standing ** skew) + 1 for standing in range(2, count + 1)]
    spare, given = total - most - (count - 1), [1] * (count - 1)
    while spare > 0:
        movable = [i for i in range(count - 1) if given[i] < most]
        pool, left = sum([portions[i] for i in movable]), spare
        for i in movable:
            addition = min(most - given[i], max(1, left * portions[i] // pool), spare)
            given[i] = given[i] + addition
            spare = spare - addition
    return np.array([most] + given)


def ragged(key, count, total, limit, slope):
    if count == 2:
        one = jax.random.randint(key, (), max(1, total - limit), min(limit, total - 1) + 1)
        return jnp.stack([one, total - one])
    sizes = jnp.asarray(split_up(count, total, limit, slope), jnp.int32)
    twos = (count - 1) // 2
    giver, sink = sizes[1:1 + 2 * twos:2], sizes[2:2 + 2 * twos:2]
    room = jnp.minimum(giver - 1, limit - sink)
    moved = jax.random.randint(jax.random.fold_in(key, 1), (twos,), 0, 1 << 20) % (room + 1)
    sizes = sizes.at[1:1 + 2 * twos:2].set(giver - moved).at[2:2 + 2 * twos:2].set(sink + moved)
    return sizes[jax.random.permutation(jax.random.fold_in(key, 2), count)]


def noise(own_key, shape, deviation, limit, shards=(), held_as=jnp.bfloat16):
    drawn = jax.random.normal(own_key, shape, jnp.float32) * deviation
    if len(shards) > 0:
        drawn = block_scale(own_key, shape, shards, -0.22, 0.18) * drawn
    return jnp.clip(drawn, min=-limit, max=limit).astype(held_as)


def heavy_noise(rng, extent, spread, reach, cuts, heavy, kind=jnp.bfloat16):
    result = spread * jax.random.normal(rng, extent, jnp.float32)
    if cuts:
        result = result * block_scale(rng, extent, cuts, -0.22, 0.18)
    return jnp.clip(spiked(result, jax.random.fold_in(rng, 3), *heavy), -reach, reach).astype(kind)


def setup_inputs(seed: int = 0) -> dict:
    splits = jax.random.split(jax.random.key(seed), 7)
    query = draw_query(jax.random.fold_in(splits[6], 71), 0)
    key_states = draw_key_states(jax.random.fold_in(splits[6], 71), 0)
    value_states = noise(splits[2], (SEQ, HEADS * HEAD_DIM), 1.0, 6.0, ((0, 128), (1, 8)))
    doc_ids = jnp.searchsorted(jnp.cumsum(ragged(splits[3], DOCS, SEQ, DOC_MOST, 1)), jnp.arange(SEQ), side="right").astype(jnp.int32)
    out_weight = heavy_noise(splits[4], (HEADS * HEAD_DIM, D), (HEADS * HEAD_DIM) ** -0.5, 0.5, ((0, 8), (1, 128)), (0, 1, 128, 5.5))
    residual = noise(splits[5], (SEQ, D), 1.0, 6.0, ((0, 128), (1, 8)))
    return {"query": query, "key_states": key_states, "value_states": value_states, "doc_ids": doc_ids, "out_weight": out_weight, "residual": residual}


masked_score = -1.0e30


def reference(query, key_states, value_states, doc_ids, out_weight, residual):
    positions = jnp.arange(SEQ, dtype=jnp.int32)
    allowed = (positions[None, :] <= positions[:, None]) & (doc_ids[None, :] == doc_ids[:, None])
    query_heads = query.reshape(SEQ, HEADS, HEAD_DIM).transpose(1, 0, 2)
    key_heads = key_states.reshape(SEQ, HEADS, HEAD_DIM).transpose(1, 0, 2)
    value_heads = value_states.reshape(SEQ, HEADS, HEAD_DIM).transpose(1, 0, 2)

    def one_head(operands):
        queries, keys, values = operands
        scores = jnp.dot(queries, keys.T, preferred_element_type=jnp.float32) * (HEAD_DIM ** -0.5)
        scores = jnp.where(allowed, scores, masked_score)
        row_max = jnp.max(scores, axis=1, keepdims=True)
        weights = jnp.where(allowed, jnp.exp(scores - row_max), 0.0)
        row_sum = jnp.sum(weights, axis=1, keepdims=True)
        attended = jnp.dot(weights.astype(jnp.bfloat16), values, preferred_element_type=jnp.float32) / row_sum
        return attended.astype(jnp.bfloat16)

    per_head = lax.map(one_head, (query_heads, key_heads, value_heads))
    attended = per_head.transpose(1, 0, 2).reshape(SEQ, HEADS * HEAD_DIM)
    mixed = residual.astype(jnp.float32) + jnp.dot(attended, out_weight, preferred_element_type=jnp.float32)
    return mixed.astype(jnp.bfloat16)
```

```python
import jax
import jax.numpy as jnp
from jax import lax
from jax.experimental import pallas as pl
from jax.experimental.pallas import tpu as pltpu
from jax.sharding import Mesh, PartitionSpec as P

HEAD_DIM = 128
BLOCK = 64
LANES = 128
ROWS = 128
HIDDEN = -1e30
LOWEST = -1e29
LOG2_E = 1.4426950408889634

AXES = (("zh", 8), ("zp", 2), ("z2", 2), ("y", 4), ("x", 4), ("c", 2))
SEQ_AXES = ("zh", "zp", "z2", "y")
HEAD_AXES = ("x", "c")
PLANES = ("zh", "zp")
KEY_AXES = ("y", "x")
QUERY_AXES = ("z2", "c")


def exchange(tiles, axes):
    return lax.all_to_all(tiles, axes, split_axis=0, concat_axis=0, tiled=True)


def gather(block, axes):
    return exchange(jnp.broadcast_to(block[None], (lax.axis_size(axes), *block.shape)), axes)


def transposed(row):
    return jnp.broadcast_to(row, (LANES, LANES)).T


def attend_kernel(place_ref, query_ref, key_ref, out_ref, score_ref):
    z2, y, x, c = (place_ref[k] for k in range(4))
    stripe = 2 * BLOCK * 4

    def positions(z2, y, x, c, dim):
        index = lax.broadcasted_iota(jnp.int32, (ROWS, LANES), dim)
        return (z2 * 4 + y) * BLOCK + 16 * x + 8 * c + (index >> 3) * stripe + (index & 7)

    sources = key_ref.shape[0]
    factor = HEAD_DIM ** (-0.5) * LOG2_E
    for r in range(query_ref.shape[0]):
        queries = query_ref[r, 0:ROWS, :]
        query_docs = transposed(query_ref[r, ROWS : ROWS + 16, :].astype(jnp.float32)[0:1])
        query_pos = positions(r // 2, y, x, r % 2, 0)
        highest = jnp.full((ROWS, LANES), HIDDEN, jnp.float32)
        for s in range(sources):
            scores = lax.dot_general(
                queries,
                key_ref[s, 0:ROWS, :],
                (((1,), (1,)), ((), ())),
                preferred_element_type=jnp.float32,
            )
            key_docs = key_ref[s, 2 * ROWS : 2 * ROWS + 16, :].astype(jnp.float32)[0:1]
            key_pos = positions(z2, s // 4, s % 4, c, 1)
            visible = (key_pos <= query_pos) & (key_docs == query_docs)
            scores = jnp.where(visible, scores, HIDDEN)
            score_ref[s] = scores
            highest = jnp.maximum(highest, scores)
        row_max = jnp.maximum(jnp.max(highest, axis=1, keepdims=True), LOWEST)
        row_max = jnp.broadcast_to(row_max, (ROWS, LANES))
        total = jnp.zeros((ROWS, LANES), jnp.float32)
        mixed = jnp.zeros((ROWS, HEAD_DIM), jnp.float32)
        for s in range(sources):
            weights = jnp.exp2((score_ref[s] - row_max) * factor)
            total = total + weights
            mixed = mixed + jnp.dot(
                weights.astype(jnp.bfloat16),
                key_ref[s, ROWS : 2 * ROWS, :],
                preferred_element_type=jnp.float32,
            )
        row_sum = jnp.broadcast_to(jnp.sum(total, axis=1, keepdims=True), (ROWS, LANES))
        out_ref[r, 0:ROWS, :] = mixed
        out_ref[r, ROWS : ROWS + 8, :] = jnp.concatenate([row_max.T[0:4], row_sum.T[0:4]], axis=0)


def combine_kernel(part_ref, out_ref):
    parts = part_ref.shape[0]
    factor = HEAD_DIM ** (-0.5) * LOG2_E
    maxima = [part_ref[r, ROWS : ROWS + 1, :] for r in range(parts)]
    sums = [part_ref[r, ROWS + 4 : ROWS + 5, :] for r in range(parts)]
    row_max = maxima[0]
    for m in maxima[1:]:
        row_max = jnp.maximum(row_max, m)
    scales = [jnp.exp2((m - row_max) * factor) for m in maxima]
    row_sum = sum(scale * s for scale, s in zip(scales, sums))
    mixed = jnp.zeros((ROWS, HEAD_DIM), jnp.float32)
    for r in range(parts):
        mixed = mixed + part_ref[r, 0:ROWS, :] * transposed(scales[r] / row_sum)
    out_ref[...] = mixed.astype(out_ref.dtype)


def attend(place, queries, keys):
    parts = queries.shape[0]
    vmem = pl.BlockSpec(memory_space=pltpu.VMEM)
    return pl.pallas_call(
        attend_kernel,
        out_shape=jax.ShapeDtypeStruct((parts, ROWS + 8, LANES), jnp.float32),
        in_specs=[pl.BlockSpec(memory_space=pltpu.SMEM), vmem, vmem],
        out_specs=vmem,
        scratch_shapes=[pltpu.VMEM((keys.shape[0], ROWS, LANES), jnp.float32)],
        compiler_params=pltpu.CompilerParams(vmem_limit_bytes=24 << 20),
        cost_estimate=pl.CostEstimate(
            flops=4 * parts * ROWS * keys.shape[0] * ROWS * HEAD_DIM,
            bytes_accessed=4 << 20,
            transcendentals=parts * ROWS * keys.shape[0] * ROWS,
        ),
        name="attend",
    )(place, queries, keys)


def combine(parts):
    vmem = pl.BlockSpec(memory_space=pltpu.VMEM)
    return pl.pallas_call(
        combine_kernel,
        out_shape=jax.ShapeDtypeStruct((ROWS, HEAD_DIM), jnp.bfloat16),
        in_specs=[vmem],
        out_specs=vmem,
        compiler_params=pltpu.CompilerParams(vmem_limit_bytes=8 << 20),
        name="combine",
    )(parts)


def weight_columns(out_weight):
    own = out_weight.T
    columns, rows = own.shape
    by_zh = gather(own, "zh")
    by_head = exchange(by_zh, HEAD_AXES)
    by_zl = gather(by_head, ("zp", "z2"))
    zl, groups = by_zl.shape[:2]
    block = by_zl.transpose(0, 2, 1, 3).reshape(zl * columns, groups * rows)
    by_y = gather(block, "y").reshape(4, zl, columns, groups * rows)
    return by_y.transpose(1, 0, 2, 3).reshape(zl * 4 * columns, groups * rows)


def shards(query, key_states, value_states, doc_ids, out_weight, residual):
    groups = lax.axis_size(HEAD_AXES)
    planes = lax.axis_size(PLANES)
    each = BLOCK // groups
    x, c = lax.axis_index("x"), lax.axis_index("c")
    place = jnp.stack([lax.axis_index("z2"), lax.axis_index("y"), x, c])

    cut = [a.reshape(groups, each, -1) for a in (query, key_states, value_states)]
    by_rows = exchange(jnp.concatenate(cut, axis=1), HEAD_AXES)
    by_rows = by_rows.reshape(groups, 3 * each, 2, HEAD_DIM).transpose(0, 2, 1, 3)
    lane = jnp.arange(LANES, dtype=jnp.int32)
    chosen = jnp.arange(BLOCK)[:, None] == ((2 * x + c) * each + lane % each)[None, :]
    docs = jnp.sum(jnp.where(chosen, doc_ids[:, None], 0), axis=0).astype(jnp.bfloat16)
    docs = jnp.broadcast_to(docs, (planes, each, LANES))
    sent = jnp.concatenate([by_rows.reshape(planes, 3 * each, HEAD_DIM), docs], axis=1)
    by_head = exchange(sent, PLANES)
    queries, keys, values = (
        by_head[:, k * each : (k + 1) * each].reshape(ROWS, HEAD_DIM) for k in range(3)
    )
    mine = (lane // each)[None, :] == jnp.arange(planes)[:, None]
    row_docs = jnp.sum(
        jnp.where(mine, by_head[:, 3 * each].astype(jnp.float32), 0.0), axis=0
    ).astype(jnp.bfloat16)
    row_docs = jnp.broadcast_to(row_docs, (16, LANES))

    all_keys = gather(jnp.concatenate([keys, values, row_docs], axis=0), KEY_AXES)
    all_queries = gather(jnp.concatenate([queries, row_docs], axis=0), QUERY_AXES)
    parts = attend(place, all_queries, all_keys)
    attended = combine(exchange(parts, QUERY_AXES))

    back = exchange(attended.reshape(planes, each, HEAD_DIM), PLANES)
    everyone = gather(back, HEAD_AXES)
    everyone = everyone.transpose(0, 2, 1, 3).reshape(BLOCK, planes * HEAD_DIM)
    weight = weight_columns(out_weight)
    summed = lax.dot_general(
        everyone, weight, (((1,), (1,)), ((), ())), preferred_element_type=jnp.float32
    )
    return (residual.astype(jnp.float32) + summed).astype(jnp.bfloat16)


def solution(mesh):
    names, sizes = zip(*AXES)
    fine = Mesh(mesh.devices.reshape(sizes), names)
    seq, head = SEQ_AXES, HEAD_AXES
    placed = (P(seq, head), P(seq, head), P(seq, head), P(seq), P(head, seq), P(seq, head))
    return jax.shard_map(
        shards, mesh=fine, in_specs=placed, out_specs=P(seq, head), check_vma=False
    )
```

```python
import itertools

import jax
import jax.numpy as jnp
from jax import lax
from jax.experimental import pallas as pl
from jax.experimental.pallas import tpu as pltpu
from jax.sharding import Mesh, PartitionSpec as P

HEAD_DIM = 128
BLOCK = 64
LANES = 128
EACH = 8
ROWS = 128
COLUMNS = 32
HIDDEN = -1e30
LOWEST = -1e29
FACTOR = HEAD_DIM ** (-0.5) * 1.4426950408889634

AXES = (("zh", 8), ("zp", 2), ("z2", 2), ("y", 4), ("x", 4), ("c", 2))
SEQ_AXES = ("zh", "zp", "z2", "y")
HEAD_AXES = ("x", "c")
PLANES = ("zh", "zp")
QUERY_AXES = ("z2", "y")

VMEM = pl.BlockSpec(memory_space=pltpu.VMEM)
SMEM = pl.BlockSpec(memory_space=pltpu.SMEM)


def exchange(tiles, axes):
    return lax.all_to_all(tiles, axes, split_axis=0, concat_axis=0, tiled=True)


def moved(block, where):
    sizes = (32, 4, 4, 2)
    places = itertools.product(*map(range, sizes))

    def flat(z, y, x, c):
        return ((z * 4 + y) * 4 + x) * 2 + c

    names = tuple(name for name, _ in AXES)
    return lax.ppermute(block, names, [(flat(*p), flat(*where(*p))) for p in places])


def transposed(row):
    return jnp.broadcast_to(row, (LANES, LANES)).T


def call(kernel, out_shape, in_specs, name, scratch=(), flops=0, moved_bytes=1 << 20):
    many = isinstance(out_shape, (list, tuple))
    return pl.pallas_call(
        kernel,
        out_shape=out_shape,
        in_specs=in_specs,
        out_specs=[VMEM] * len(out_shape) if many else VMEM,
        scratch_shapes=list(scratch),
        compiler_params=pltpu.CompilerParams(vmem_limit_bytes=24 << 20),
        cost_estimate=pl.CostEstimate(flops=flops, bytes_accessed=moved_bytes, transcendentals=0),
        name=name,
    )


WEIGHT_AT = 4 * EACH
SENT = WEIGHT_AT + 2 * COLUMNS


def send_kernel(rows_ref, docs_ref, weight_ref, out_ref):
    docs = jnp.broadcast_to(docs_ref[...].astype(jnp.float32), (EACH, LANES))
    weight = [weight_ref[:, k * LANES : (k + 1) * LANES] for k in range(2)]
    for group in range(rows_ref.shape[0]):
        for j in range(2):
            lanes = slice(j * LANES, (j + 1) * LANES)
            values = rows_ref[group, 2 * EACH : 3 * EACH, lanes].astype(jnp.float32)
            tile = out_ref.at[2 * group + j]
            tile[0 : 2 * EACH, :] = rows_ref[group, 0 : 2 * EACH, lanes]
            tile[2 * EACH : 4 * EACH, :] = jnp.concatenate([values, docs], axis=0).astype(
                jnp.bfloat16
            )
            for k in range(2):
                at = WEIGHT_AT + k * COLUMNS
                tile[at : at + COLUMNS, :] = weight[k]


DOCS_AT = 2 * ROWS
COLUMNS_AT = DOCS_AT + 16
GATHERED = COLUMNS_AT + 4 * COLUMNS


def gather_kernel(place_ref, came_ref, query_ref, key_ref):
    planes = came_ref.shape[0]
    first = [came_ref[i, 0 : 2 * EACH, :].astype(jnp.float32) for i in range(planes)]
    second = [came_ref[i, 2 * EACH : 4 * EACH, :].astype(jnp.float32) for i in range(planes)]
    queries, keys = (
        jnp.concatenate([t[k * EACH : (k + 1) * EACH] for t in first], axis=0).astype(jnp.bfloat16)
        for k in range(2)
    )
    values = jnp.concatenate([t[0:EACH] for t in second], axis=0).astype(jnp.bfloat16)
    lane = lax.broadcasted_iota(jnp.int32, (EACH, LANES), 1)
    docs = jnp.zeros((EACH, LANES), jnp.float32)
    for i, tile in enumerate(second):
        own = pltpu.roll(tile[EACH:], EACH * i, 1)
        docs = jnp.where(lane // EACH == i, own, docs)
    docs = jnp.concatenate([docs, docs], axis=0).astype(jnp.bfloat16)
    for s in range(query_ref.shape[0]):
        query_ref[s, 0:ROWS, :] = queries
        query_ref[s, ROWS : ROWS + 16, :] = docs
    for s in range(key_ref.shape[0]):
        key_ref[s, 0:ROWS, :] = keys
        key_ref[s, ROWS:DOCS_AT, :] = values
        key_ref[s, DOCS_AT:COLUMNS_AT, :] = docs
        for k in range(2):
            at = COLUMNS_AT + k * 2 * COLUMNS
            key_ref[s, at : at + 2 * COLUMNS, :] = came_ref[2 * s + k, WEIGHT_AT:SENT, :]


def attend_kernel(place_ref, query_ref, key_ref, out_ref, score_ref):
    z2, y, x, c = (place_ref[k] for k in range(1, 5))
    stripe = 2 * BLOCK * 4

    def positions(z2, y, x, c, dim):
        index = lax.broadcasted_iota(jnp.int32, (ROWS, LANES), dim)
        first = (z2 * 4 + y) * BLOCK + EACH * (2 * x + c)
        return first + (index >> 3) * stripe + (index & 7)

    sources = key_ref.shape[0]
    for r in range(query_ref.shape[0]):
        queries = query_ref[r, 0:ROWS, :]
        query_docs = transposed(query_ref[r, ROWS : ROWS + 16, :].astype(jnp.float32)[0:1])
        query_pos = positions(r // 4, r % 4, x, c, 0)
        highest = jnp.full((ROWS, LANES), HIDDEN, jnp.float32)
        for s in range(sources):
            scores = lax.dot_general(
                queries,
                key_ref[s, 0:ROWS, :],
                (((1,), (1,)), ((), ())),
                preferred_element_type=jnp.float32,
            )
            key_docs = key_ref[s, DOCS_AT:COLUMNS_AT, :].astype(jnp.float32)[0:1]
            key_pos = positions(z2, y, s // 2, s % 2, 1)
            visible = (key_pos <= query_pos) & (key_docs == query_docs)
            scores = jnp.where(visible, scores, HIDDEN)
            score_ref[s] = scores
            highest = jnp.maximum(highest, scores)
        row_max = jnp.maximum(jnp.max(highest, axis=1, keepdims=True), LOWEST)
        row_max = jnp.broadcast_to(row_max, (ROWS, LANES))
        total = jnp.zeros((ROWS, LANES), jnp.float32)
        mixed = jnp.zeros((ROWS, HEAD_DIM), jnp.float32)
        for s in range(sources):
            weights = jnp.exp2((score_ref[s] - row_max) * FACTOR)
            total = total + weights
            mixed = mixed + jnp.dot(
                weights.astype(jnp.bfloat16),
                key_ref[s, ROWS:DOCS_AT, :],
                preferred_element_type=jnp.float32,
            )
        row_sum = jnp.broadcast_to(jnp.sum(total, axis=1, keepdims=True), (ROWS, LANES))
        out_ref[r, 0:ROWS, :] = mixed
        out_ref[r, ROWS : ROWS + 8, :] = jnp.concatenate([row_max.T[0:4], row_sum.T[0:4]], axis=0)


def combine_kernel(part_ref, out_ref):
    parts = part_ref.shape[0]
    maxima = [part_ref[r, ROWS : ROWS + 1, :] for r in range(parts)]
    sums = [part_ref[r, ROWS + 4 : ROWS + 5, :] for r in range(parts)]
    row_max = maxima[0]
    for m in maxima[1:]:
        row_max = jnp.maximum(row_max, m)
    scales = [jnp.exp2((m - row_max) * FACTOR) for m in maxima]
    row_sum = sum(scale * s for scale, s in zip(scales, sums))
    mixed = jnp.zeros((ROWS, HEAD_DIM), jnp.float32)
    for r in range(parts):
        mixed = mixed + part_ref[r, 0:ROWS, :] * transposed(scales[r] / row_sum)
    out_ref[...] = mixed.astype(out_ref.dtype)


def product_kernel(place_ref, attended_ref, w0, w1, w2, w3, residual_ref, out_ref):
    z2, y = place_ref[1], place_ref[2]
    total = jnp.zeros(out_ref.shape, jnp.float32)
    for p in range(attended_ref.shape[0]):
        heads = [
            attended_ref[:, 2 * p + j].astype(jnp.float32).reshape(BLOCK, HEAD_DIM)
            for j in range(2)
        ]
        left = jnp.concatenate(heads, axis=1).astype(jnp.bfloat16)
        blocks = []
        for zl in range(4):
            own = (zl & 1) ^ z2
            for w in (w0, w1, w2, w3):
                halves = []
                for k in range(2):
                    at = ((zl >> 1) * 2 + k) * COLUMNS
                    halves.append(w[own, p, at : at + COLUMNS, :])
                blocks.append(jnp.concatenate(halves, axis=1))
        total = total + lax.dot_general(
            left,
            jnp.concatenate(blocks, axis=0),
            (((1,), (1,)), ((), ())),
            preferred_element_type=jnp.float32,
        )
    for zl in range(4):
        columns = slice(zl * LANES, (zl + 1) * LANES)
        summed = pltpu.roll(total[:, columns], y * COLUMNS, 1)
        out_ref[:, columns] = (residual_ref[:, columns].astype(jnp.float32) + summed).astype(
            out_ref.dtype
        )


def shards(query, key_states, value_states, doc_ids, out_weight, residual):
    groups = lax.axis_size(HEAD_AXES)
    planes = lax.axis_size(PLANES)
    spread = lax.axis_size(QUERY_AXES)
    bf16, f32 = jnp.bfloat16, jnp.float32
    index = [lax.axis_index(a) for a in (PLANES, "z2", "y", "x", "c")]
    place = jnp.stack(index)

    cut = [a.reshape(groups, EACH, -1) for a in (query, key_states, value_states)]
    by_rows = exchange(jnp.concatenate(cut, axis=1), HEAD_AXES)
    first = (2 * lax.axis_index("x") + lax.axis_index("c")) * EACH
    docs = jnp.roll(doc_ids, -first)
    docs = jnp.concatenate([docs, docs]).astype(bf16).reshape(1, LANES)
    sent = call(
        send_kernel, jax.ShapeDtypeStruct((planes, SENT, LANES), bf16), [VMEM] * 3, "send"
    )(by_rows, docs, out_weight.T)
    came = exchange(sent, PLANES)
    queries, keys = call(
        gather_kernel,
        [
            jax.ShapeDtypeStruct((spread, ROWS + 16, LANES), bf16),
            jax.ShapeDtypeStruct((groups, GATHERED, LANES), bf16),
        ],
        [SMEM, VMEM],
        "spread",
    )(place, came)
    keys = exchange(keys, HEAD_AXES)
    queries = exchange(queries, QUERY_AXES)

    columns = keys[:, COLUMNS_AT:]
    columns = jnp.stack([columns, moved(columns, lambda z, y, x, c: (z ^ 1, y, x, c))])
    weights = [columns]
    weights += [moved(columns, lambda z, y, x, c: (z, (y - k) % 4, x, c)) for k in (1, 2, 3)]

    parts = call(
        attend_kernel,
        jax.ShapeDtypeStruct((spread, ROWS + 8, LANES), f32),
        [SMEM, VMEM, VMEM],
        "attend",
        [pltpu.VMEM((groups, ROWS, LANES), f32)],
        4 * spread * ROWS * groups * ROWS * HEAD_DIM,
        2 << 20,
    )(place, queries, keys)
    parts = exchange(parts, QUERY_AXES)
    attended = call(
        combine_kernel, jax.ShapeDtypeStruct((ROWS, HEAD_DIM), bf16), [VMEM], "combine"
    )(parts)

    back = exchange(attended.reshape(planes, EACH, HEAD_DIM), PLANES)
    everyone = exchange(jnp.broadcast_to(back[None], (groups, *back.shape)), HEAD_AXES)
    return call(
        product_kernel,
        jax.ShapeDtypeStruct(residual.shape, residual.dtype),
        [SMEM] + [VMEM] * 6,
        "product",
        (),
        2 * BLOCK * 2048 * 512,
        3 << 20,
    )(place, everyone, *weights, residual)


def solution(mesh):
    names, sizes = zip(*AXES)
    fine = Mesh(mesh.devices.reshape(sizes), names)
    seq, head = SEQ_AXES, HEAD_AXES
    placed = (P(seq, head), P(seq, head), P(seq, head), P(seq), P(head, seq), P(seq, head))
    return jax.shard_map(
        shards, mesh=fine, in_specs=placed, out_specs=P(seq, head), check_vma=False
    )
```

```python
import itertools

import jax
import jax.numpy as jnp
from jax import lax
from jax.experimental import pallas as pl
from jax.experimental.pallas import tpu as pltpu
from jax.sharding import Mesh, PartitionSpec as P

HEAD_DIM = 128
BLOCK = 64
LANES = 128
EACH = 8
ROWS = 128
COLUMNS = 32
HIDDEN = -1e30
LOWEST = -1e29
FACTOR = HEAD_DIM ** (-0.5) * 1.4426950408889634

AXES = (("zh", 8), ("zp", 2), ("z2", 2), ("y", 4), ("x", 4), ("c", 2))
SEQ_AXES = ("zh", "zp", "z2", "y")
HEAD_AXES = ("x", "c")
PLANES = ("zh", "zp")
QUERY_AXES = ("z2", "y")

VMEM = pl.BlockSpec(memory_space=pltpu.VMEM)
SMEM = pl.BlockSpec(memory_space=pltpu.SMEM)


def exchange(tiles, axes):
    return lax.all_to_all(tiles, axes, split_axis=0, concat_axis=0, tiled=True)


def moved(block, where):
    sizes = (32, 4, 4, 2)
    places = itertools.product(*map(range, sizes))

    def flat(z, y, x, c):
        return ((z * 4 + y) * 4 + x) * 2 + c

    names = tuple(name for name, _ in AXES)
    return lax.ppermute(block, names, [(flat(*p), flat(*where(*p))) for p in places])


def transposed(row):
    return jnp.broadcast_to(row, (LANES, LANES)).T


def call(kernel, out_shape, in_specs, name, scratch=(), flops=0, moved_bytes=1 << 20):
    many = isinstance(out_shape, (list, tuple))
    return pl.pallas_call(
        kernel,
        out_shape=out_shape,
        in_specs=in_specs,
        out_specs=[VMEM] * len(out_shape) if many else VMEM,
        scratch_shapes=list(scratch),
        compiler_params=pltpu.CompilerParams(vmem_limit_bytes=24 << 20),
        cost_estimate=pl.CostEstimate(flops=flops, bytes_accessed=moved_bytes, transcendentals=0),
        name=name,
    )


WEIGHT_AT = 4 * EACH
SENT = WEIGHT_AT + COLUMNS


def send_kernel(rows_ref, docs_ref, weight_ref, out_ref):
    docs = jnp.broadcast_to(docs_ref[...].astype(jnp.float32), (EACH, LANES))
    weight = [weight_ref[:, k * LANES : (k + 1) * LANES] for k in range(2)]
    for group in range(rows_ref.shape[0]):
        for j in range(2):
            lanes = slice(j * LANES, (j + 1) * LANES)
            values = rows_ref[group, 2 * EACH : 3 * EACH, lanes].astype(jnp.float32)
            tile = out_ref.at[2 * group + j]
            tile[0 : 2 * EACH, :] = rows_ref[group, 0 : 2 * EACH, lanes]
            tile[2 * EACH : 4 * EACH, :] = jnp.concatenate([values, docs], axis=0).astype(
                jnp.bfloat16
            )
            tile[WEIGHT_AT:SENT, :] = weight[j]


DOCS_AT = 2 * ROWS
COLUMNS_AT = DOCS_AT + 16
GATHERED = COLUMNS_AT + 2 * COLUMNS


def gather_kernel(place_ref, came_ref, query_ref, key_ref):
    planes = came_ref.shape[0]
    first = [came_ref[i, 0 : 2 * EACH, :].astype(jnp.float32) for i in range(planes)]
    second = [came_ref[i, 2 * EACH : 4 * EACH, :].astype(jnp.float32) for i in range(planes)]
    queries, keys = (
        jnp.concatenate([t[k * EACH : (k + 1) * EACH] for t in first], axis=0).astype(jnp.bfloat16)
        for k in range(2)
    )
    values = jnp.concatenate([t[0:EACH] for t in second], axis=0).astype(jnp.bfloat16)
    lane = lax.broadcasted_iota(jnp.int32, (EACH, LANES), 1)
    docs = jnp.zeros((EACH, LANES), jnp.float32)
    for i, tile in enumerate(second):
        own = pltpu.roll(tile[EACH:], EACH * i, 1)
        docs = jnp.where(lane // EACH == i, own, docs)
    docs = jnp.concatenate([docs, docs], axis=0).astype(jnp.bfloat16)
    for s in range(query_ref.shape[0]):
        query_ref[s, 0:ROWS, :] = queries
        query_ref[s, ROWS : ROWS + 16, :] = docs
    for s in range(key_ref.shape[0]):
        key_ref[s, 0:ROWS, :] = keys
        key_ref[s, ROWS:DOCS_AT, :] = values
        key_ref[s, DOCS_AT:COLUMNS_AT, :] = docs
        for k in range(2):
            at = COLUMNS_AT + k * COLUMNS
            key_ref[s, at : at + COLUMNS, :] = came_ref[2 * s + k, WEIGHT_AT:SENT, :]


def attend_kernel(place_ref, query_ref, key_ref, other_ref, out_ref, columns_ref, score_ref):
    columns_ref[0] = key_ref[:, COLUMNS_AT:GATHERED, :]
    columns_ref[1] = other_ref[...]
    z2, y, x, c = (place_ref[k] for k in range(4))
    stripe = 2 * BLOCK * 4

    def positions(z2, y, x, c, dim):
        index = lax.broadcasted_iota(jnp.int32, (ROWS, LANES), dim)
        first = (z2 * 4 + y) * BLOCK + EACH * (2 * x + c)
        return first + (index >> 3) * stripe + (index & 7)

    sources = key_ref.shape[0]
    for r in range(query_ref.shape[0]):
        queries = query_ref[r, 0:ROWS, :]
        query_docs = transposed(query_ref[r, ROWS : ROWS + 16, :].astype(jnp.float32)[0:1])
        query_pos = positions(r // 4, r % 4, x, c, 0)
        highest = jnp.full((ROWS, LANES), HIDDEN, jnp.float32)
        for s in range(sources):
            scores = lax.dot_general(
                queries,
                key_ref[s, 0:ROWS, :],
                (((1,), (1,)), ((), ())),
                preferred_element_type=jnp.float32,
            )
            key_docs = key_ref[s, DOCS_AT:COLUMNS_AT, :].astype(jnp.float32)[0:1]
            key_pos = positions(z2, y, s // 2, s % 2, 1)
            visible = (key_pos <= query_pos) & (key_docs == query_docs)
            scores = jnp.where(visible, scores, HIDDEN)
            score_ref[s] = scores
            highest = jnp.maximum(highest, scores)
        row_max = jnp.maximum(jnp.max(highest, axis=1, keepdims=True), LOWEST)
        row_max = jnp.broadcast_to(row_max, (ROWS, LANES))
        total = jnp.zeros((ROWS, LANES), jnp.float32)
        mixed = jnp.zeros((ROWS, HEAD_DIM), jnp.float32)
        for s in range(sources):
            weights = jnp.exp2((score_ref[s] - row_max) * FACTOR)
            total = total + weights
            mixed = mixed + jnp.dot(
                weights.astype(jnp.bfloat16),
                key_ref[s, ROWS:DOCS_AT, :],
                preferred_element_type=jnp.float32,
            )
        row_sum = jnp.broadcast_to(jnp.sum(total, axis=1, keepdims=True), (ROWS, LANES))
        out_ref[r, 0:ROWS, :] = mixed
        out_ref[r, ROWS : ROWS + 8, :] = jnp.concatenate([row_max.T[0:4], row_sum.T[0:4]], axis=0)


def combine_kernel(part_ref, columns_ref, out_ref, same_ref):
    same_ref[...] = columns_ref[...]
    parts = part_ref.shape[0]
    maxima = [part_ref[r, ROWS : ROWS + 1, :] for r in range(parts)]
    sums = [part_ref[r, ROWS + 4 : ROWS + 5, :] for r in range(parts)]
    row_max = maxima[0]
    for m in maxima[1:]:
        row_max = jnp.maximum(row_max, m)
    scales = [jnp.exp2((m - row_max) * FACTOR) for m in maxima]
    row_sum = sum(scale * s for scale, s in zip(scales, sums))
    mixed = jnp.zeros((ROWS, HEAD_DIM), jnp.float32)
    for r in range(parts):
        mixed = mixed + part_ref[r, 0:ROWS, :] * transposed(scales[r] / row_sum)
    out_ref[...] = mixed.astype(out_ref.dtype)


def product_kernel(place_ref, attended_ref, *refs):
    weights, (residual_ref, out_ref) = refs[:8], refs[8:]
    z2, y, zp = place_ref[0], place_ref[1], place_ref[4]
    total = jnp.zeros(out_ref.shape, jnp.float32)
    for p in range(attended_ref.shape[0]):
        heads = [
            attended_ref[:, 2 * p + j].astype(jnp.float32).reshape(BLOCK, HEAD_DIM)
            for j in range(2)
        ]
        left = jnp.concatenate(heads, axis=1).astype(jnp.bfloat16)
        blocks = []
        for k in range(2):
            rows = slice(k * COLUMNS, (k + 1) * COLUMNS)
            for w in weights:
                halves = [w[zp ^ j, p, rows, :] for j in range(2)]
                blocks.append(jnp.concatenate(halves, axis=1))
        total = total + lax.dot_general(
            left,
            jnp.concatenate(blocks, axis=0),
            (((1,), (1,)), ((), ())),
            preferred_element_type=jnp.float32,
        )
    for k in range(2):
        own, other = (
            pltpu.roll(total[:, at : at + LANES], y * COLUMNS, 1)
            for at in (2 * k * LANES, (2 * k + 1) * LANES)
        )
        for j in range(2):
            columns = slice((2 * k + j) * LANES, (2 * k + j + 1) * LANES)
            summed = jnp.where(z2 == j, own, other)
            out_ref[:, columns] = (residual_ref[:, columns].astype(jnp.float32) + summed).astype(
                out_ref.dtype
            )


def shards(query, key_states, value_states, doc_ids, out_weight, residual):
    groups = lax.axis_size(HEAD_AXES)
    planes = lax.axis_size(PLANES)
    spread = lax.axis_size(QUERY_AXES)
    bf16, f32 = jnp.bfloat16, jnp.float32
    index = [lax.axis_index(a) for a in ("z2", "y", "x", "c", "zp")]
    place = jnp.stack(index)

    cut = [a.reshape(groups, EACH, -1) for a in (query, key_states, value_states)]
    by_rows = exchange(jnp.concatenate(cut, axis=1), HEAD_AXES)
    first = (2 * lax.axis_index("x") + lax.axis_index("c")) * EACH
    docs = jnp.roll(doc_ids, -first)
    docs = jnp.concatenate([docs, docs]).astype(bf16).reshape(1, LANES)
    sent = call(
        send_kernel, jax.ShapeDtypeStruct((planes, SENT, LANES), bf16), [VMEM] * 3, "send"
    )(by_rows, docs, out_weight.T)
    came = exchange(sent, PLANES)
    queries, keys = call(
        gather_kernel,
        [
            jax.ShapeDtypeStruct((spread, ROWS + 16, LANES), bf16),
            jax.ShapeDtypeStruct((groups, GATHERED, LANES), bf16),
        ],
        [SMEM, VMEM],
        "spread",
    )(place, came)
    keys = exchange(keys, HEAD_AXES)
    queries = exchange(queries, QUERY_AXES)

    columns = keys[:, COLUMNS_AT:]
    columns = moved(columns, lambda z, y, x, c: (z ^ 2, y, x, c))
    held = jax.ShapeDtypeStruct((2, *columns.shape), bf16)

    def every_y(block):
        return [block] + [
            moved(block, lambda z, y, x, c: (z, (y - k) % 4, x, c)) for k in (1, 2, 3)
        ]

    parts, columns = call(
        attend_kernel,
        [jax.ShapeDtypeStruct((spread, ROWS + 8, LANES), f32), held],
        [SMEM] + [VMEM] * 3,
        "attend",
        [pltpu.VMEM((groups, ROWS, LANES), f32)],
        4 * spread * ROWS * groups * ROWS * HEAD_DIM,
        2 << 20,
    )(place, queries, keys, columns)
    parts = exchange(parts, QUERY_AXES)
    weights = every_y(columns)
    attended, columns = call(
        combine_kernel,
        [jax.ShapeDtypeStruct((ROWS, HEAD_DIM), bf16), held],
        [VMEM] * 2,
        "combine",
    )(parts, moved(columns, lambda z, y, x, c: (z ^ 1, y, x, c)))
    weights += every_y(columns)

    back = exchange(attended.reshape(planes, EACH, HEAD_DIM), PLANES)
    everyone = exchange(jnp.broadcast_to(back[None], (groups, *back.shape)), HEAD_AXES)
    return call(
        product_kernel,
        jax.ShapeDtypeStruct(residual.shape, residual.dtype),
        [SMEM] + [VMEM] * 10,
        "product",
        (),
        2 * BLOCK * 2048 * 512,
        3 << 20,
    )(place, everyone, *weights, residual)


def solution(mesh):
    names, sizes = zip(*AXES)
    fine = Mesh(mesh.devices.reshape(sizes), names)
    seq, head = SEQ_AXES, HEAD_AXES
    placed = (P(seq, head), P(seq, head), P(seq, head), P(seq), P(head, seq), P(seq, head))
    return jax.shard_map(
        shards, mesh=fine, in_specs=placed, out_specs=P(seq, head), check_vma=False
    )
```

```python
import itertools

import jax
import jax.numpy as jnp
from jax import lax
from jax.experimental import pallas as pl
from jax.experimental.pallas import tpu as pltpu
from jax.sharding import Mesh, PartitionSpec as P

HEAD_DIM = 128
BLOCK = 64
LANES = 128
EACH = 8
ROWS = 128
COLUMNS = 32
HIDDEN = -1e30
LOWEST = -1e29
FACTOR = HEAD_DIM ** (-0.5) * 1.4426950408889634

AXES = (("zh", 8), ("zp", 2), ("z2", 2), ("y", 4), ("x", 4), ("c", 2))
SEQ_AXES = ("zh", "zp", "z2", "y")
HEAD_AXES = ("x", "c")
PLANES = ("zh", "zp")
KEY_AXES = ("z2", "y")

VMEM = pl.BlockSpec(memory_space=pltpu.VMEM)
SMEM = pl.BlockSpec(memory_space=pltpu.SMEM)


def exchange(tiles, axes):
    return lax.all_to_all(tiles, axes, split_axis=0, concat_axis=0, tiled=True)


def moved(block, where):
    sizes = (32, 4, 4, 2)
    places = itertools.product(*map(range, sizes))

    def flat(z, y, x, c):
        return ((z * 4 + y) * 4 + x) * 2 + c

    names = tuple(name for name, _ in AXES)
    return lax.ppermute(block, names, [(flat(*p), flat(*where(*p))) for p in places])


def transposed(row):
    return jnp.broadcast_to(row, (LANES, LANES)).T


def call(kernel, out_shape, in_specs, name, scratch=(), flops=0, moved_bytes=1 << 20):
    many = isinstance(out_shape, (list, tuple))
    return pl.pallas_call(
        kernel,
        out_shape=out_shape,
        in_specs=in_specs,
        out_specs=[VMEM] * len(out_shape) if many else VMEM,
        scratch_shapes=list(scratch),
        compiler_params=pltpu.CompilerParams(vmem_limit_bytes=24 << 20),
        cost_estimate=pl.CostEstimate(flops=flops, bytes_accessed=moved_bytes, transcendentals=0),
        name=name,
    )


WEIGHT_AT = 4 * EACH
SENT = WEIGHT_AT + COLUMNS


def send_kernel(rows_ref, docs_ref, weight_ref, out_ref):
    docs = jnp.broadcast_to(docs_ref[...].astype(jnp.float32), (EACH, LANES))
    weight = [weight_ref[:, k * LANES : (k + 1) * LANES] for k in range(2)]
    for group in range(rows_ref.shape[0]):
        for j in range(2):
            lanes = slice(j * LANES, (j + 1) * LANES)
            values = rows_ref[group, 2 * EACH : 3 * EACH, lanes].astype(jnp.float32)
            tile = out_ref.at[2 * group + j]
            tile[0 : 2 * EACH, :] = rows_ref[group, 0 : 2 * EACH, lanes]
            tile[2 * EACH : 4 * EACH, :] = jnp.concatenate([values, docs], axis=0).astype(
                jnp.bfloat16
            )
            tile[WEIGHT_AT:SENT, :] = weight[j]


COLUMNS_AT = ROWS + 16
GATHERED = COLUMNS_AT + 2 * COLUMNS
DOCS_AT = 2 * ROWS


def gather_kernel(came_ref, query_ref, key_ref):
    planes = came_ref.shape[0]
    first = [came_ref[i, 0 : 2 * EACH, :].astype(jnp.float32) for i in range(planes)]
    second = [came_ref[i, 2 * EACH : 4 * EACH, :].astype(jnp.float32) for i in range(planes)]
    queries, keys = (
        jnp.concatenate([t[k * EACH : (k + 1) * EACH] for t in first], axis=0).astype(jnp.bfloat16)
        for k in range(2)
    )
    values = jnp.concatenate([t[0:EACH] for t in second], axis=0).astype(jnp.bfloat16)
    lane = lax.broadcasted_iota(jnp.int32, (EACH, LANES), 1)
    docs = jnp.zeros((EACH, LANES), jnp.float32)
    for i, tile in enumerate(second):
        docs = jnp.where(lane // EACH == i, pltpu.roll(tile[EACH:], EACH * i, 1), docs)
    docs = jnp.concatenate([docs, docs], axis=0).astype(jnp.bfloat16)
    for s in range(query_ref.shape[0]):
        query_ref[s, 0:ROWS, :] = queries
        query_ref[s, ROWS:COLUMNS_AT, :] = docs
        for k in range(2):
            at = COLUMNS_AT + k * COLUMNS
            query_ref[s, at : at + COLUMNS, :] = came_ref[2 * s + k, WEIGHT_AT:SENT, :]
    for s in range(key_ref.shape[0]):
        key_ref[s, 0:ROWS, :] = keys
        key_ref[s, ROWS:DOCS_AT, :] = values
        key_ref[s, DOCS_AT : DOCS_AT + 16, :] = docs


def attend_kernel(place_ref, query_ref, key_ref, *refs):
    by_z1, by_z2, by_z3, out_ref, own_ref, other_ref, score_ref = refs
    own_ref[0] = query_ref[:, COLUMNS_AT:GATHERED, :]
    own_ref[1] = by_z2[...]
    other_ref[0] = by_z1[...]
    other_ref[1] = by_z3[...]
    z2, y, x, c = (place_ref[k] for k in range(4))
    stripe = 2 * BLOCK * 4

    def positions(z2, y, x, c, dim):
        index = lax.broadcasted_iota(jnp.int32, (ROWS, LANES), dim)
        first = (z2 * 4 + y) * BLOCK + EACH * (2 * x + c)
        return first + (index >> 3) * stripe + (index & 7)

    sources = key_ref.shape[0]
    for r in range(query_ref.shape[0]):
        queries = query_ref[r, 0:ROWS, :]
        query_docs = transposed(query_ref[r, ROWS:COLUMNS_AT, :].astype(jnp.float32)[0:1])
        query_pos = positions(z2, y, r // 2, r % 2, 0)
        highest = jnp.full((ROWS, LANES), HIDDEN, jnp.float32)
        for s in range(sources):
            scores = lax.dot_general(
                queries,
                key_ref[s, 0:ROWS, :],
                (((1,), (1,)), ((), ())),
                preferred_element_type=jnp.float32,
            )
            key_docs = key_ref[s, DOCS_AT : DOCS_AT + 16, :].astype(jnp.float32)[0:1]
            key_pos = positions(s // 4, s % 4, x, c, 1)
            visible = (key_pos <= query_pos) & (key_docs == query_docs)
            scores = jnp.where(visible, scores, HIDDEN)
            score_ref[s] = scores
            highest = jnp.maximum(highest, scores)
        row_max = jnp.maximum(jnp.max(highest, axis=1, keepdims=True), LOWEST)
        row_max = jnp.broadcast_to(row_max, (ROWS, LANES))
        total = jnp.zeros((ROWS, LANES), jnp.float32)
        mixed = jnp.zeros((ROWS, HEAD_DIM), jnp.float32)
        for s in range(sources):
            weights = jnp.exp2((score_ref[s] - row_max) * FACTOR)
            total = total + weights
            mixed = mixed + jnp.dot(
                weights.astype(jnp.bfloat16),
                key_ref[s, ROWS:DOCS_AT, :],
                preferred_element_type=jnp.float32,
            )
        row_sum = jnp.broadcast_to(jnp.sum(total, axis=1, keepdims=True), (ROWS, LANES))
        out_ref[r, 0:ROWS, :] = mixed
        out_ref[r, ROWS : ROWS + 8, :] = jnp.concatenate([row_max.T[0:4], row_sum.T[0:4]], axis=0)


def combine_kernel(part_ref, own_ref, other_ref, out_ref, same_own_ref, same_other_ref):
    same_own_ref[...] = own_ref[...]
    same_other_ref[...] = other_ref[...]
    parts = part_ref.shape[0]
    maxima = [part_ref[r, ROWS : ROWS + 1, :] for r in range(parts)]
    sums = [part_ref[r, ROWS + 4 : ROWS + 5, :] for r in range(parts)]
    row_max = maxima[0]
    for m in maxima[1:]:
        row_max = jnp.maximum(row_max, m)
    scales = [jnp.exp2((m - row_max) * FACTOR) for m in maxima]
    row_sum = sum(scale * s for scale, s in zip(scales, sums))
    mixed = jnp.zeros((ROWS, HEAD_DIM), jnp.float32)
    for r in range(parts):
        mixed = mixed + part_ref[r, 0:ROWS, :] * transposed(scales[r] / row_sum)
    out_ref[...] = mixed.astype(out_ref.dtype)


def product_kernel(place_ref, attended_ref, *refs):
    weights, (residual_ref, out_ref) = refs[:8], refs[8:]
    z2, y, zp = place_ref[0], place_ref[1], place_ref[4]
    total = jnp.zeros(out_ref.shape, jnp.float32)
    for p in range(attended_ref.shape[0]):
        heads = [
            attended_ref[:, 2 * p + j].astype(jnp.float32).reshape(BLOCK, HEAD_DIM)
            for j in range(2)
        ]
        left = jnp.concatenate(heads, axis=1).astype(jnp.bfloat16)
        blocks = []
        for k in range(2):
            rows = slice(k * COLUMNS, (k + 1) * COLUMNS)
            for w in weights:
                halves = [w[zp ^ j, p, rows, :] for j in range(2)]
                blocks.append(jnp.concatenate(halves, axis=1))
        total = total + lax.dot_general(
            left,
            jnp.concatenate(blocks, axis=0),
            (((1,), (1,)), ((), ())),
            preferred_element_type=jnp.float32,
        )
    for k in range(2):
        own, other = (
            pltpu.roll(total[:, at : at + LANES], y * COLUMNS, 1)
            for at in (2 * k * LANES, (2 * k + 1) * LANES)
        )
        for j in range(2):
            columns = slice((2 * k + j) * LANES, (2 * k + j + 1) * LANES)
            summed = jnp.where(z2 == j, own, other)
            out_ref[:, columns] = (residual_ref[:, columns].astype(jnp.float32) + summed).astype(
                out_ref.dtype
            )


def shards(query, key_states, value_states, doc_ids, out_weight, residual):
    groups = lax.axis_size(HEAD_AXES)
    planes = lax.axis_size(PLANES)
    spread = lax.axis_size(KEY_AXES)
    bf16, f32 = jnp.bfloat16, jnp.float32
    index = [lax.axis_index(a) for a in ("z2", "y", "x", "c", "zp")]
    place = jnp.stack(index)

    cut = [a.reshape(groups, EACH, -1) for a in (query, key_states, value_states)]
    by_rows = exchange(jnp.concatenate(cut, axis=1), HEAD_AXES)
    first = (2 * lax.axis_index("x") + lax.axis_index("c")) * EACH
    docs = jnp.roll(doc_ids, -first)
    docs = jnp.concatenate([docs, docs]).astype(bf16).reshape(1, LANES)
    sent = call(
        send_kernel, jax.ShapeDtypeStruct((planes, SENT, LANES), bf16), [VMEM] * 3, "send"
    )(by_rows, docs, out_weight.T)
    came = exchange(sent, PLANES)
    queries, keys = call(
        gather_kernel,
        [
            jax.ShapeDtypeStruct((groups, GATHERED, LANES), bf16),
            jax.ShapeDtypeStruct((spread, DOCS_AT + 16, LANES), bf16),
        ],
        [VMEM],
        "spread",
    )(came)
    queries = exchange(queries, HEAD_AXES)
    keys = exchange(keys, KEY_AXES)

    columns = queries[:, COLUMNS_AT:]
    near = [moved(columns, lambda z, y, x, c: (z ^ far, y, x, c)) for far in (1, 2, 3)]
    held = jax.ShapeDtypeStruct((2, *columns.shape), bf16)

    def from_y(block, k):
        return moved(block, lambda z, y, x, c: (z, (y - k) % 4, x, c))

    parts, own, other = call(
        attend_kernel,
        [jax.ShapeDtypeStruct((groups, ROWS + 8, LANES), f32), held, held],
        [SMEM] + [VMEM] * 5,
        "attend",
        [pltpu.VMEM((spread, ROWS, LANES), f32)],
        4 * spread * ROWS * groups * ROWS * HEAD_DIM,
        2 << 20,
    )(place, queries, keys, *near)
    parts = exchange(parts, HEAD_AXES)
    next_own, last_own = from_y(own, 1), from_y(own, 3)
    attended, own, other = call(
        combine_kernel,
        [jax.ShapeDtypeStruct((ROWS, HEAD_DIM), bf16), held, held],
        [VMEM] * 3,
        "combine",
    )(parts, own, other)
    weights = [own, next_own, from_y(own, 2), last_own]
    weights += [other] + [from_y(other, k) for k in (1, 2, 3)]

    back = exchange(attended.reshape(planes, EACH, HEAD_DIM), PLANES)
    everyone = exchange(jnp.broadcast_to(back[None], (groups, *back.shape)), HEAD_AXES)
    return call(
        product_kernel,
        jax.ShapeDtypeStruct(residual.shape, residual.dtype),
        [SMEM] + [VMEM] * 10,
        "product",
        (),
        2 * BLOCK * 2048 * 512,
        3 << 20,
    )(place, everyone, *weights, residual)


def solution(mesh):
    names, sizes = zip(*AXES)
    fine = Mesh(mesh.devices.reshape(sizes), names)
    seq, head = SEQ_AXES, HEAD_AXES
    placed = (P(seq, head), P(seq, head), P(seq, head), P(seq), P(head, seq), P(seq, head))
    return jax.shard_map(
        shards, mesh=fine, in_specs=placed, out_specs=P(seq, head), check_vma=False
    )
```

```python
import itertools

import jax
import jax.numpy as jnp
from jax import lax
from jax.experimental import pallas as pl
from jax.experimental.pallas import tpu as pltpu
from jax.sharding import Mesh, PartitionSpec as P

HEAD_DIM = 128
BLOCK = 64
LANES = 128
EACH = 8
ROWS = 128
COLUMNS = 32
HIDDEN = -1e30
LOWEST = -1e29
FACTOR = HEAD_DIM ** (-0.5) * 1.4426950408889634

AXES = (("zh", 8), ("zp", 2), ("z2", 2), ("y", 4), ("x", 4), ("c", 2))
SEQ_AXES = ("zh", "zp", "z2", "y")
HEAD_AXES = ("x", "c")
PLANES = ("zh", "zp")
QUERY_AXES = ("z2", "y")

VMEM = pl.BlockSpec(memory_space=pltpu.VMEM)
SMEM = pl.BlockSpec(memory_space=pltpu.SMEM)


def exchange(tiles, axes):
    return lax.all_to_all(tiles, axes, split_axis=0, concat_axis=0, tiled=True)


def moved(block, where):
    sizes = (32, 4, 4, 2)
    places = itertools.product(*map(range, sizes))

    def flat(z, y, x, c):
        return ((z * 4 + y) * 4 + x) * 2 + c

    names = tuple(name for name, _ in AXES)
    return lax.ppermute(block, names, [(flat(*p), flat(*where(*p))) for p in places])


def transposed(row):
    return jnp.broadcast_to(row, (LANES, LANES)).T


def call(kernel, out_shape, in_specs, name, scratch=(), flops=0, moved_bytes=1 << 20):
    many = isinstance(out_shape, (list, tuple))
    return pl.pallas_call(
        kernel,
        out_shape=out_shape,
        in_specs=in_specs,
        out_specs=[VMEM] * len(out_shape) if many else VMEM,
        scratch_shapes=list(scratch),
        compiler_params=pltpu.CompilerParams(vmem_limit_bytes=24 << 20),
        cost_estimate=pl.CostEstimate(flops=flops, bytes_accessed=moved_bytes, transcendentals=0),
        name=name,
    )


WEIGHT_AT = 4 * EACH
SENT = WEIGHT_AT + COLUMNS


def send_kernel(rows_ref, docs_ref, weight_ref, out_ref):
    docs = jnp.broadcast_to(docs_ref[...].astype(jnp.float32), (EACH, LANES))
    weight = [weight_ref[:, k * LANES : (k + 1) * LANES] for k in range(2)]
    for group in range(rows_ref.shape[0]):
        for j in range(2):
            lanes = slice(j * LANES, (j + 1) * LANES)
            values = rows_ref[group, 2 * EACH : 3 * EACH, lanes].astype(jnp.float32)
            tile = out_ref.at[2 * group + j]
            tile[0 : 2 * EACH, :] = rows_ref[group, 0 : 2 * EACH, lanes]
            tile[2 * EACH : 4 * EACH, :] = jnp.concatenate([values, docs], axis=0).astype(
                jnp.bfloat16
            )
            tile[WEIGHT_AT:SENT, :] = weight[j]


DOCS_AT = 2 * ROWS
COLUMNS_AT = DOCS_AT + 16
GATHERED = COLUMNS_AT + 2 * COLUMNS


def gather_kernel(came_ref, query_ref, key_ref):
    planes = came_ref.shape[0]
    first = [came_ref[i, 0 : 2 * EACH, :].astype(jnp.float32) for i in range(planes)]
    second = [came_ref[i, 2 * EACH : 4 * EACH, :].astype(jnp.float32) for i in range(planes)]
    queries, keys = (
        jnp.concatenate([t[k * EACH : (k + 1) * EACH] for t in first], axis=0).astype(jnp.bfloat16)
        for k in range(2)
    )
    values = jnp.concatenate([t[0:EACH] for t in second], axis=0).astype(jnp.bfloat16)
    lane = lax.broadcasted_iota(jnp.int32, (EACH, LANES), 1)
    docs = jnp.zeros((EACH, LANES), jnp.float32)
    for i, tile in enumerate(second):
        docs = jnp.where(lane // EACH == i, pltpu.roll(tile[EACH:], EACH * i, 1), docs)
    docs = jnp.concatenate([docs, docs], axis=0).astype(jnp.bfloat16)
    query_ref[0:ROWS, :] = queries
    query_ref[ROWS : ROWS + 16, :] = docs
    for s in range(key_ref.shape[0]):
        key_ref[s, 0:ROWS, :] = keys
        key_ref[s, ROWS:DOCS_AT, :] = values
        key_ref[s, DOCS_AT:COLUMNS_AT, :] = docs
        for k in range(2):
            at = COLUMNS_AT + k * COLUMNS
            key_ref[s, at : at + COLUMNS, :] = came_ref[2 * s + k, WEIGHT_AT:SENT, :]


def attend_kernel(place_ref, query_ref, key_ref, out_ref, score_ref):
    z2, y, x, c = (place_ref[k] for k in range(4))
    stripe = 2 * BLOCK * 4

    def positions(z2, y, x, c, dim):
        index = lax.broadcasted_iota(jnp.int32, (ROWS, LANES), dim)
        first = (z2 * 4 + y) * BLOCK + EACH * (2 * x + c)
        return first + (index >> 3) * stripe + (index & 7)

    sources = key_ref.shape[0]
    for r in range(query_ref.shape[0]):
        queries = query_ref[r, 0:ROWS, :]
        query_docs = transposed(query_ref[r, ROWS : ROWS + 16, :].astype(jnp.float32)[0:1])
        query_pos = positions(r // 4, r % 4, x, c, 0)
        highest = jnp.full((ROWS, LANES), HIDDEN, jnp.float32)
        for s in range(sources):
            scores = lax.dot_general(
                queries,
                key_ref[s, 0:ROWS, :],
                (((1,), (1,)), ((), ())),
                preferred_element_type=jnp.float32,
            )
            key_docs = key_ref[s, DOCS_AT:COLUMNS_AT, :].astype(jnp.float32)[0:1]
            key_pos = positions(z2, y, s // 2, s % 2, 1)
            visible = (key_pos <= query_pos) & (key_docs == query_docs)
            scores = jnp.where(visible, scores, HIDDEN)
            score_ref[s] = scores
            highest = jnp.maximum(highest, scores)
        row_max = jnp.maximum(jnp.max(highest, axis=1, keepdims=True), LOWEST)
        row_max = jnp.broadcast_to(row_max, (ROWS, LANES))
        total = jnp.zeros((ROWS, LANES), jnp.float32)
        mixed = jnp.zeros((ROWS, HEAD_DIM), jnp.float32)
        for s in range(sources):
            weights = jnp.exp2((score_ref[s] - row_max) * FACTOR)
            total = total + weights
            mixed = mixed + jnp.dot(
                weights.astype(jnp.bfloat16),
                key_ref[s, ROWS:DOCS_AT, :],
                preferred_element_type=jnp.float32,
            )
        row_sum = jnp.broadcast_to(jnp.sum(total, axis=1, keepdims=True), (ROWS, LANES))
        out_ref[r, 0:ROWS, :] = mixed
        out_ref[r, ROWS : ROWS + 8, :] = jnp.concatenate([row_max.T[0:4], row_sum.T[0:4]], axis=0)


def combine_kernel(part_ref, key_ref, by_z1, by_z2, by_z3, out_ref, own_ref, other_ref):
    own_ref[0] = key_ref[:, COLUMNS_AT:GATHERED, :]
    own_ref[1] = by_z2[...]
    other_ref[0] = by_z1[...]
    other_ref[1] = by_z3[...]
    parts = part_ref.shape[0]
    maxima = [part_ref[r, ROWS : ROWS + 1, :] for r in range(parts)]
    sums = [part_ref[r, ROWS + 4 : ROWS + 5, :] for r in range(parts)]
    row_max = maxima[0]
    for m in maxima[1:]:
        row_max = jnp.maximum(row_max, m)
    scales = [jnp.exp2((m - row_max) * FACTOR) for m in maxima]
    row_sum = sum(scale * s for scale, s in zip(scales, sums))
    mixed = jnp.zeros((ROWS, HEAD_DIM), jnp.float32)
    for r in range(parts):
        mixed = mixed + part_ref[r, 0:ROWS, :] * transposed(scales[r] / row_sum)
    out_ref[...] = mixed.astype(out_ref.dtype)


def product_kernel(place_ref, attended_ref, *refs):
    weights, (residual_ref, out_ref) = refs[:8], refs[8:]
    z2, y, zp = place_ref[0], place_ref[1], place_ref[4]
    total = jnp.zeros(out_ref.shape, jnp.float32)
    for p in range(attended_ref.shape[0]):
        heads = [
            attended_ref[:, 2 * p + j].astype(jnp.float32).reshape(BLOCK, HEAD_DIM)
            for j in range(2)
        ]
        left = jnp.concatenate(heads, axis=1).astype(jnp.bfloat16)
        blocks = []
        for k in range(2):
            rows = slice(k * COLUMNS, (k + 1) * COLUMNS)
            for w in weights:
                halves = [w[zp ^ j, p, rows, :] for j in range(2)]
                blocks.append(jnp.concatenate(halves, axis=1))
        total = total + lax.dot_general(
            left,
            jnp.concatenate(blocks, axis=0),
            (((1,), (1,)), ((), ())),
            preferred_element_type=jnp.float32,
        )
    for k in range(2):
        own, other = (
            pltpu.roll(total[:, at : at + LANES], y * COLUMNS, 1)
            for at in (2 * k * LANES, (2 * k + 1) * LANES)
        )
        for j in range(2):
            columns = slice((2 * k + j) * LANES, (2 * k + j + 1) * LANES)
            summed = jnp.where(z2 == j, own, other)
            out_ref[:, columns] = (residual_ref[:, columns].astype(jnp.float32) + summed).astype(
                out_ref.dtype
            )


def shards(query, key_states, value_states, doc_ids, out_weight, residual):
    groups = lax.axis_size(HEAD_AXES)
    planes = lax.axis_size(PLANES)
    spread = lax.axis_size(QUERY_AXES)
    bf16, f32 = jnp.bfloat16, jnp.float32
    index = [lax.axis_index(a) for a in ("z2", "y", "x", "c", "zp")]
    place = jnp.stack(index)

    cut = [a.reshape(groups, EACH, -1) for a in (query, key_states, value_states)]
    by_rows = exchange(jnp.concatenate(cut, axis=1), HEAD_AXES)
    first = (2 * lax.axis_index("x") + lax.axis_index("c")) * EACH
    docs = jnp.roll(doc_ids, -first)
    docs = jnp.concatenate([docs, docs]).astype(bf16).reshape(1, LANES)
    sent = call(
        send_kernel, jax.ShapeDtypeStruct((planes, SENT, LANES), bf16), [VMEM] * 3, "send"
    )(by_rows, docs, out_weight.T)
    came = exchange(sent, PLANES)
    queries, keys = call(
        gather_kernel,
        [
            jax.ShapeDtypeStruct((ROWS + 16, LANES), bf16),
            jax.ShapeDtypeStruct((groups, GATHERED, LANES), bf16),
        ],
        [VMEM],
        "spread",
    )(came)
    keys = exchange(keys, HEAD_AXES)
    queries = lax.all_gather(queries, QUERY_AXES)

    parts = call(
        attend_kernel,
        jax.ShapeDtypeStruct((spread, ROWS + 8, LANES), f32),
        [SMEM] + [VMEM] * 2,
        "attend",
        [pltpu.VMEM((groups, ROWS, LANES), f32)],
        4 * spread * ROWS * groups * ROWS * HEAD_DIM,
        2 << 20,
    )(place, queries, keys)
    parts = exchange(parts, QUERY_AXES)

    columns = keys[:, COLUMNS_AT:]
    near = [moved(columns, lambda z, y, x, c: (z ^ far, y, x, c)) for far in (1, 2, 3)]
    held = jax.ShapeDtypeStruct((2, *columns.shape), bf16)
    attended, own, other = call(
        combine_kernel,
        [jax.ShapeDtypeStruct((ROWS, HEAD_DIM), bf16), held, held],
        [VMEM] * 5,
        "combine",
    )(parts, keys, *near)

    def from_y(block, k):
        return moved(block, lambda z, y, x, c: (z, (y - k) % 4, x, c))

    weights = [own] + [from_y(own, k) for k in (1, 2, 3)]
    weights += [other] + [from_y(other, k) for k in (1, 2, 3)]

    back = exchange(attended.reshape(planes, EACH, HEAD_DIM), PLANES)
    everyone = exchange(jnp.broadcast_to(back[None], (groups, *back.shape)), HEAD_AXES)
    return call(
        product_kernel,
        jax.ShapeDtypeStruct(residual.shape, residual.dtype),
        [SMEM] + [VMEM] * 10,
        "product",
        (),
        2 * BLOCK * 2048 * 512,
        3 << 20,
    )(place, everyone, *weights, residual)


def solution(mesh):
    names, sizes = zip(*AXES)
    fine = Mesh(mesh.devices.reshape(sizes), names)
    seq, head = SEQ_AXES, HEAD_AXES
    placed = (P(seq, head), P(seq, head), P(seq, head), P(seq), P(head, seq), P(seq, head))
    return jax.shard_map(
        shards, mesh=fine, in_specs=placed, out_specs=P(seq, head), check_vma=False
    )
```

```python
import itertools

import jax
import jax.numpy as jnp
from jax import lax
from jax.experimental import pallas as pl
from jax.experimental.pallas import tpu as pltpu
from jax.sharding import Mesh, PartitionSpec as P

HEAD_DIM = 128
BLOCK = 64
LANES = 128
EACH = 8
ROWS = 128
COLUMNS = 32
HIDDEN = -1e30
LOWEST = -1e29
FACTOR = HEAD_DIM ** (-0.5) * 1.4426950408889634

AXES = (("zh", 8), ("zp", 2), ("z2", 2), ("y", 4), ("x", 4), ("c", 2))
SEQ_AXES = ("zh", "zp", "z2", "y")
HEAD_AXES = ("x", "c")
PLANES = ("zh", "zp")
KEY_AXES = ("z2", "x", "c")
QUERY_AXES = ("y",)

VMEM = pl.BlockSpec(memory_space=pltpu.VMEM)
SMEM = pl.BlockSpec(memory_space=pltpu.SMEM)


def exchange(tiles, axes):
    return lax.all_to_all(tiles, axes, split_axis=0, concat_axis=0, tiled=True)


def moved(block, where):
    sizes = (32, 4, 4, 2)
    places = itertools.product(*map(range, sizes))

    def flat(z, y, x, c):
        return ((z * 4 + y) * 4 + x) * 2 + c

    names = tuple(name for name, _ in AXES)
    return lax.ppermute(block, names, [(flat(*p), flat(*where(*p))) for p in places])


def transposed(row):
    return jnp.broadcast_to(row, (LANES, LANES)).T


def call(kernel, out_shape, in_specs, name, scratch=(), flops=0, moved_bytes=1 << 20):
    many = isinstance(out_shape, (list, tuple))
    return pl.pallas_call(
        kernel,
        out_shape=out_shape,
        in_specs=in_specs,
        out_specs=[VMEM] * len(out_shape) if many else VMEM,
        scratch_shapes=list(scratch),
        compiler_params=pltpu.CompilerParams(vmem_limit_bytes=24 << 20),
        cost_estimate=pl.CostEstimate(flops=flops, bytes_accessed=moved_bytes, transcendentals=0),
        name=name,
    )


WEIGHT_AT = 4 * EACH
SENT = WEIGHT_AT + COLUMNS


def send_kernel(rows_ref, docs_ref, weight_ref, out_ref):
    docs = jnp.broadcast_to(docs_ref[...].astype(jnp.float32), (EACH, LANES))
    weight = [weight_ref[:, k * LANES : (k + 1) * LANES] for k in range(2)]
    for group in range(rows_ref.shape[0]):
        for j in range(2):
            lanes = slice(j * LANES, (j + 1) * LANES)
            values = rows_ref[group, 2 * EACH : 3 * EACH, lanes].astype(jnp.float32)
            tile = out_ref.at[2 * group + j]
            tile[0 : 2 * EACH, :] = rows_ref[group, 0 : 2 * EACH, lanes]
            tile[2 * EACH : 4 * EACH, :] = jnp.concatenate([values, docs], axis=0).astype(
                jnp.bfloat16
            )
            tile[WEIGHT_AT:SENT, :] = weight[j]


DOCS_AT = 2 * ROWS
COLUMNS_AT = DOCS_AT + 16
GATHERED = COLUMNS_AT + 2 * COLUMNS


def gather_kernel(came_ref, query_ref, key_ref):
    planes = came_ref.shape[0]
    first = [came_ref[i, 0 : 2 * EACH, :].astype(jnp.float32) for i in range(planes)]
    second = [came_ref[i, 2 * EACH : 4 * EACH, :].astype(jnp.float32) for i in range(planes)]
    queries, keys = (
        jnp.concatenate([t[k * EACH : (k + 1) * EACH] for t in first], axis=0).astype(jnp.bfloat16)
        for k in range(2)
    )
    values = jnp.concatenate([t[0:EACH] for t in second], axis=0).astype(jnp.bfloat16)
    lane = lax.broadcasted_iota(jnp.int32, (EACH, LANES), 1)
    docs = jnp.zeros((EACH, LANES), jnp.float32)
    for i, tile in enumerate(second):
        docs = jnp.where(lane // EACH == i, pltpu.roll(tile[EACH:], EACH * i, 1), docs)
    docs = jnp.concatenate([docs, docs], axis=0).astype(jnp.bfloat16)
    query_ref[0:ROWS, :] = queries
    query_ref[ROWS : ROWS + 16, :] = docs
    for s in range(key_ref.shape[0]):
        key_ref[s, 0:ROWS, :] = keys
        key_ref[s, ROWS:DOCS_AT, :] = values
        key_ref[s, DOCS_AT:COLUMNS_AT, :] = docs
        for k in range(2):
            at = COLUMNS_AT + k * COLUMNS
            key_ref[s, at : at + COLUMNS, :] = came_ref[2 * (s % 8) + k, WEIGHT_AT:SENT, :]


def attend_kernel(place_ref, query_ref, key_ref, out_ref, score_ref):
    z2, y, x, c = (place_ref[k] for k in range(4))
    stripe = 2 * BLOCK * 4

    def positions(z2, y, x, c, dim):
        index = lax.broadcasted_iota(jnp.int32, (ROWS, LANES), dim)
        first = (z2 * 4 + y) * BLOCK + EACH * (2 * x + c)
        return first + (index >> 3) * stripe + (index & 7)

    sources = key_ref.shape[0]
    for r in range(query_ref.shape[0]):
        queries = query_ref[r, 0:ROWS, :]
        query_docs = transposed(query_ref[r, ROWS : ROWS + 16, :].astype(jnp.float32)[0:1])
        query_pos = positions(z2, r, x, c, 0)
        highest = jnp.full((ROWS, LANES), HIDDEN, jnp.float32)
        for s in range(sources):
            scores = lax.dot_general(
                queries,
                key_ref[s, 0:ROWS, :],
                (((1,), (1,)), ((), ())),
                preferred_element_type=jnp.float32,
            )
            key_docs = key_ref[s, DOCS_AT:COLUMNS_AT, :].astype(jnp.float32)[0:1]
            key_pos = positions(s // 8, y, s % 8 // 2, s % 2, 1)
            visible = (key_pos <= query_pos) & (key_docs == query_docs)
            scores = jnp.where(visible, scores, HIDDEN)
            score_ref[s] = scores
            highest = jnp.maximum(highest, scores)
        row_max = jnp.maximum(jnp.max(highest, axis=1, keepdims=True), LOWEST)
        row_max = jnp.broadcast_to(row_max, (ROWS, LANES))
        total = jnp.zeros((ROWS, LANES), jnp.float32)
        mixed = jnp.zeros((ROWS, HEAD_DIM), jnp.float32)
        for s in range(sources):
            weights = jnp.exp2((score_ref[s] - row_max) * FACTOR)
            total = total + weights
            mixed = mixed + jnp.dot(
                weights.astype(jnp.bfloat16),
                key_ref[s, ROWS:DOCS_AT, :],
                preferred_element_type=jnp.float32,
            )
        row_sum = jnp.broadcast_to(jnp.sum(total, axis=1, keepdims=True), (ROWS, LANES))
        out_ref[r, 0:ROWS, :] = mixed
        out_ref[r, ROWS : ROWS + 8, :] = jnp.concatenate([row_max.T[0:4], row_sum.T[0:4]], axis=0)


def columns_kernel(key_ref, after_ref, out_ref):
    out_ref[...] = key_ref[:, COLUMNS_AT:GATHERED, :]


def combine_kernel(part_ref, own_ref, other_ref, out_ref, same_own_ref, same_other_ref):
    same_own_ref[...] = own_ref[...]
    same_other_ref[...] = other_ref[...]
    parts = part_ref.shape[0]
    maxima = [part_ref[r, ROWS : ROWS + 1, :] for r in range(parts)]
    sums = [part_ref[r, ROWS + 4 : ROWS + 5, :] for r in range(parts)]
    row_max = maxima[0]
    for m in maxima[1:]:
        row_max = jnp.maximum(row_max, m)
    scales = [jnp.exp2((m - row_max) * FACTOR) for m in maxima]
    row_sum = sum(scale * s for scale, s in zip(scales, sums))
    mixed = jnp.zeros((ROWS, HEAD_DIM), jnp.float32)
    for r in range(parts):
        mixed = mixed + part_ref[r, 0:ROWS, :] * transposed(scales[r] / row_sum)
    out_ref[...] = mixed.astype(out_ref.dtype)


def product_kernel(place_ref, attended_ref, *refs):
    weights, (residual_ref, out_ref) = refs[:8], refs[8:]
    y, zp = place_ref[1], place_ref[4]
    groups = attended_ref.shape[0]
    total = jnp.zeros(out_ref.shape, jnp.float32)
    for p in range(groups):
        heads = [
            attended_ref[:, 2 * p + (zp ^ j)].astype(jnp.float32).reshape(BLOCK, HEAD_DIM)
            for j in range(2)
        ]
        left = jnp.concatenate(heads, axis=1).astype(jnp.bfloat16)
        blocks = []
        for k in range(2):
            rows = slice(k * COLUMNS, (k + 1) * COLUMNS)
            for z2 in range(2):
                for own, other in zip(weights[:4], weights[4:]):
                    halves = [w[z2 * groups + p, rows, :] for w in (own, other)]
                    blocks.append(jnp.concatenate(halves, axis=1))
        total = total + lax.dot_general(
            left,
            jnp.concatenate(blocks, axis=0),
            (((1,), (1,)), ((), ())),
            preferred_element_type=jnp.float32,
        )
    for zl in range(4):
        columns = slice(zl * LANES, (zl + 1) * LANES)
        summed = pltpu.roll(total[:, columns], y * COLUMNS, 1)
        out_ref[:, columns] = (residual_ref[:, columns].astype(jnp.float32) + summed).astype(
            out_ref.dtype
        )


def shards(query, key_states, value_states, doc_ids, out_weight, residual):
    groups = lax.axis_size(HEAD_AXES)
    planes = lax.axis_size(PLANES)
    spread = lax.axis_size(QUERY_AXES)
    sources = lax.axis_size(KEY_AXES)
    bf16, f32 = jnp.bfloat16, jnp.float32
    index = [lax.axis_index(a) for a in ("z2", "y", "x", "c", "zp")]
    place = jnp.stack(index)

    cut = [a.reshape(groups, EACH, -1) for a in (query, key_states, value_states)]
    by_rows = exchange(jnp.concatenate(cut, axis=1), HEAD_AXES)
    first = (2 * lax.axis_index("x") + lax.axis_index("c")) * EACH
    docs = jnp.roll(doc_ids, -first)
    docs = jnp.concatenate([docs, docs]).astype(bf16).reshape(1, LANES)
    sent = call(
        send_kernel, jax.ShapeDtypeStruct((planes, SENT, LANES), bf16), [VMEM] * 3, "send"
    )(by_rows, docs, out_weight.T)
    came = exchange(sent, PLANES)
    queries, keys = call(
        gather_kernel,
        [
            jax.ShapeDtypeStruct((ROWS + 16, LANES), bf16),
            jax.ShapeDtypeStruct((sources, GATHERED, LANES), bf16),
        ],
        [VMEM],
        "spread",
    )(came)
    keys = exchange(keys, KEY_AXES)
    queries = lax.all_gather(queries, QUERY_AXES)

    parts = call(
        attend_kernel,
        jax.ShapeDtypeStruct((spread, ROWS + 8, LANES), f32),
        [SMEM] + [VMEM] * 2,
        "attend",
        [pltpu.VMEM((sources, ROWS, LANES), f32)],
        4 * spread * ROWS * sources * ROWS * HEAD_DIM,
        2 << 20,
    )(place, queries, keys)
    parts = exchange(parts, QUERY_AXES)

    def from_y(block, k):
        return moved(block, lambda z, y, x, c: (z, (y - k) % 4, x, c))

    held = jax.ShapeDtypeStruct((sources, GATHERED - COLUMNS_AT, LANES), bf16)
    own = call(columns_kernel, held, [VMEM, pl.BlockSpec(memory_space=pl.ANY)], "columns")(
        keys, queries
    )
    other = moved(own, lambda z, y, x, c: (z ^ 2, y, x, c))
    far = from_y(own, 2)
    attended, own, other = call(
        combine_kernel,
        [jax.ShapeDtypeStruct((ROWS, HEAD_DIM), bf16), held, held],
        [VMEM] * 3,
        "combine",
    )(parts, own, other)
    weights = [own, from_y(own, 1), far, from_y(own, 3)]
    weights += [other] + [from_y(other, k) for k in (1, 2, 3)]

    back = exchange(attended.reshape(planes, EACH, HEAD_DIM), PLANES)
    everyone = exchange(jnp.broadcast_to(back[None], (groups, *back.shape)), HEAD_AXES)
    return call(
        product_kernel,
        jax.ShapeDtypeStruct(residual.shape, residual.dtype),
        [SMEM] + [VMEM] * 10,
        "product",
        (),
        2 * BLOCK * 2048 * 512,
        3 << 20,
    )(place, everyone, *weights, residual)


def solution(mesh):
    names, sizes = zip(*AXES)
    fine = Mesh(mesh.devices.reshape(sizes), names)
    seq, head = SEQ_AXES, HEAD_AXES
    placed = (P(seq, head), P(seq, head), P(seq, head), P(seq), P(head, seq), P(seq, head))
    return jax.shard_map(
        shards, mesh=fine, in_specs=placed, out_specs=P(seq, head), check_vma=False
    )
```

```python
import itertools

import jax
import jax.numpy as jnp
from jax import lax
from jax.experimental import pallas as pl
from jax.experimental.pallas import tpu as pltpu
from jax.sharding import Mesh, PartitionSpec as P

HEAD_DIM = 128
BLOCK = 64
LANES = 128
EACH = 8
ROWS = 128
COLUMNS = 32
HIDDEN = -1e30
LOWEST = -1e29
FACTOR = HEAD_DIM ** (-0.5) * 1.4426950408889634

AXES = (("zh", 8), ("zp", 2), ("z2", 2), ("y", 4), ("x", 4), ("c", 2))
SEQ_AXES = ("zh", "zp", "z2", "y")
HEAD_AXES = ("x", "c")
PLANES = ("zh", "zp")
KEY_AXES = ("z2", "x", "c")
QUERY_AXES = ("y",)

VMEM = pl.BlockSpec(memory_space=pltpu.VMEM)
SMEM = pl.BlockSpec(memory_space=pltpu.SMEM)


def exchange(tiles, axes):
    return lax.all_to_all(tiles, axes, split_axis=0, concat_axis=0, tiled=True)


def moved(block, where):
    sizes = (32, 4, 4, 2)
    places = itertools.product(*map(range, sizes))

    def flat(z, y, x, c):
        return ((z * 4 + y) * 4 + x) * 2 + c

    names = tuple(name for name, _ in AXES)
    return lax.ppermute(block, names, [(flat(*p), flat(*where(*p))) for p in places])


def transposed(row):
    return jnp.broadcast_to(row, (LANES, LANES)).T


def call(kernel, out_shape, in_specs, name, scratch=(), flops=0, moved_bytes=1 << 20):
    many = isinstance(out_shape, (list, tuple))
    return pl.pallas_call(
        kernel,
        out_shape=out_shape,
        in_specs=in_specs,
        out_specs=[VMEM] * len(out_shape) if many else VMEM,
        scratch_shapes=list(scratch),
        compiler_params=pltpu.CompilerParams(vmem_limit_bytes=24 << 20),
        cost_estimate=pl.CostEstimate(flops=flops, bytes_accessed=moved_bytes, transcendentals=0),
        name=name,
    )


WEIGHT_AT = 4 * EACH
SENT = WEIGHT_AT + COLUMNS


def send_kernel(rows_ref, docs_ref, weight_ref, out_ref):
    docs = jnp.broadcast_to(docs_ref[...].astype(jnp.float32), (EACH, LANES))
    weight = [weight_ref[:, k * LANES : (k + 1) * LANES] for k in range(2)]
    for group in range(rows_ref.shape[0]):
        for j in range(2):
            lanes = slice(j * LANES, (j + 1) * LANES)
            values = rows_ref[group, 2 * EACH : 3 * EACH, lanes].astype(jnp.float32)
            tile = out_ref.at[2 * group + j]
            tile[0 : 2 * EACH, :] = rows_ref[group, 0 : 2 * EACH, lanes]
            tile[2 * EACH : 4 * EACH, :] = jnp.concatenate([values, docs], axis=0).astype(
                jnp.bfloat16
            )
            tile[WEIGHT_AT:SENT, :] = weight[j]


DOCS_AT = 2 * ROWS
COLUMNS_AT = DOCS_AT + 16
GATHERED = COLUMNS_AT + 2 * COLUMNS


def gather_kernel(came_ref, query_ref, key_ref):
    planes = came_ref.shape[0]
    first = [came_ref[i, 0 : 2 * EACH, :].astype(jnp.float32) for i in range(planes)]
    second = [came_ref[i, 2 * EACH : 4 * EACH, :].astype(jnp.float32) for i in range(planes)]
    queries, keys = (
        jnp.concatenate([t[k * EACH : (k + 1) * EACH] for t in first], axis=0).astype(jnp.bfloat16)
        for k in range(2)
    )
    values = jnp.concatenate([t[0:EACH] for t in second], axis=0).astype(jnp.bfloat16)
    lane = lax.broadcasted_iota(jnp.int32, (EACH, LANES), 1)
    docs = jnp.zeros((EACH, LANES), jnp.float32)
    for i, tile in enumerate(second):
        docs = jnp.where(lane // EACH == i, pltpu.roll(tile[EACH:], EACH * i, 1), docs)
    docs = jnp.concatenate([docs, docs], axis=0).astype(jnp.bfloat16)
    query_ref[0:ROWS, :] = queries
    query_ref[ROWS : ROWS + 16, :] = docs
    for s in range(key_ref.shape[0]):
        key_ref[s, 0:ROWS, :] = keys
        key_ref[s, ROWS:DOCS_AT, :] = values
        key_ref[s, DOCS_AT:COLUMNS_AT, :] = docs
        for k in range(2):
            at = COLUMNS_AT + k * COLUMNS
            key_ref[s, at : at + COLUMNS, :] = came_ref[2 * (s % 8) + k, WEIGHT_AT:SENT, :]


def attend_kernel(place_ref, query_ref, key_ref, out_ref, score_ref):
    z2, y, x, c = (place_ref[k] for k in range(4))
    stripe = 2 * BLOCK * 4

    def positions(z2, y, x, c, dim):
        index = lax.broadcasted_iota(jnp.int32, (ROWS, LANES), dim)
        first = (z2 * 4 + y) * BLOCK + EACH * (2 * x + c)
        return first + (index >> 3) * stripe + (index & 7)

    sources = key_ref.shape[0]
    key_docs = [
        key_ref[s, DOCS_AT:COLUMNS_AT, :].astype(jnp.float32)[0:1] for s in range(sources)
    ]
    key_pos = [positions(s // 8, y, s % 8 // 2, s % 2, 1)[0:1] for s in range(sources)]
    for first in range(0, query_ref.shape[0], 2):
        pair = (first, first + 1)
        queries = jnp.concatenate([query_ref[r, 0:ROWS, :] for r in pair], axis=0)
        query_docs = jnp.concatenate(
            [
                transposed(query_ref[r, ROWS : ROWS + 16, :].astype(jnp.float32)[0:1])
                for r in pair
            ],
            axis=0,
        )
        query_pos = jnp.concatenate([positions(z2, r, x, c, 0) for r in pair], axis=0)
        shape = query_pos.shape
        highest = jnp.full(shape, HIDDEN, jnp.float32)
        for s in range(sources):
            scores = lax.dot_general(
                queries,
                key_ref[s, 0:ROWS, :],
                (((1,), (1,)), ((), ())),
                preferred_element_type=jnp.float32,
            )
            visible = (key_pos[s] <= query_pos) & (key_docs[s] == query_docs)
            scores = jnp.where(visible, scores, HIDDEN)
            score_ref[s] = scores
            highest = jnp.maximum(highest, scores)
        row_max = jnp.maximum(jnp.max(highest, axis=1, keepdims=True), LOWEST)
        row_max = jnp.broadcast_to(row_max, shape)
        total = jnp.zeros(shape, jnp.float32)
        mixed = jnp.zeros(shape, jnp.float32)
        for s in range(0, sources, 2):
            weights, values = [], []
            for k in (s, s + 1):
                weight = jnp.exp2((score_ref[k] - row_max) * FACTOR)
                total = total + weight
                weights.append(weight.astype(jnp.bfloat16))
                values.append(key_ref[k, ROWS:DOCS_AT, :])
            mixed = mixed + jnp.dot(
                jnp.concatenate(weights, axis=1),
                jnp.concatenate(values, axis=0),
                preferred_element_type=jnp.float32,
            )
        row_sum = jnp.broadcast_to(jnp.sum(total, axis=1, keepdims=True), shape)
        for k, r in enumerate(pair):
            rows = slice(k * ROWS, (k + 1) * ROWS)
            out_ref[r, 0:ROWS, :] = mixed[rows]
            out_ref[r, ROWS : ROWS + 8, :] = jnp.concatenate(
                [row_max[rows].T[0:4], row_sum[rows].T[0:4]], axis=0
            )


def columns_kernel(key_ref, after_ref, out_ref):
    out_ref[...] = key_ref[:, COLUMNS_AT:GATHERED, :]


def combine_kernel(part_ref, own_ref, other_ref, out_ref, same_own_ref, same_other_ref):
    same_own_ref[...] = own_ref[...]
    same_other_ref[...] = other_ref[...]
    parts = part_ref.shape[0]
    maxima = [part_ref[r, ROWS : ROWS + 1, :] for r in range(parts)]
    sums = [part_ref[r, ROWS + 4 : ROWS + 5, :] for r in range(parts)]
    row_max = maxima[0]
    for m in maxima[1:]:
        row_max = jnp.maximum(row_max, m)
    scales = [jnp.exp2((m - row_max) * FACTOR) for m in maxima]
    row_sum = sum(scale * s for scale, s in zip(scales, sums))
    mixed = jnp.zeros((ROWS, HEAD_DIM), jnp.float32)
    for r in range(parts):
        mixed = mixed + part_ref[r, 0:ROWS, :] * transposed(scales[r] / row_sum)
    out_ref[...] = mixed.astype(out_ref.dtype)


def product_kernel(place_ref, attended_ref, *refs):
    weights, (residual_ref, out_ref) = refs[:8], refs[8:]
    y, zp = place_ref[1], place_ref[4]
    groups = attended_ref.shape[0]
    total = jnp.zeros(out_ref.shape, jnp.float32)
    for p in range(groups):
        heads = [
            attended_ref[:, 2 * p + (zp ^ j)].astype(jnp.float32).reshape(BLOCK, HEAD_DIM)
            for j in range(2)
        ]
        left = jnp.concatenate(heads, axis=1).astype(jnp.bfloat16)
        blocks = []
        for k in range(2):
            rows = slice(k * COLUMNS, (k + 1) * COLUMNS)
            for z2 in range(2):
                for own, other in zip(weights[:4], weights[4:]):
                    halves = [w[z2 * groups + p, rows, :] for w in (own, other)]
                    blocks.append(jnp.concatenate(halves, axis=1))
        total = total + lax.dot_general(
            left,
            jnp.concatenate(blocks, axis=0),
            (((1,), (1,)), ((), ())),
            preferred_element_type=jnp.float32,
        )
    for zl in range(4):
        columns = slice(zl * LANES, (zl + 1) * LANES)
        summed = pltpu.roll(total[:, columns], y * COLUMNS, 1)
        out_ref[:, columns] = (residual_ref[:, columns].astype(jnp.float32) + summed).astype(
            out_ref.dtype
        )


def shards(query, key_states, value_states, doc_ids, out_weight, residual):
    groups = lax.axis_size(HEAD_AXES)
    planes = lax.axis_size(PLANES)
    spread = lax.axis_size(QUERY_AXES)
    sources = lax.axis_size(KEY_AXES)
    bf16, f32 = jnp.bfloat16, jnp.float32
    index = [lax.axis_index(a) for a in ("z2", "y", "x", "c", "zp")]
    place = jnp.stack(index)

    cut = [a.reshape(groups, EACH, -1) for a in (query, key_states, value_states)]
    by_rows = exchange(jnp.concatenate(cut, axis=1), HEAD_AXES)
    first = (2 * lax.axis_index("x") + lax.axis_index("c")) * EACH
    docs = jnp.roll(doc_ids, -first)
    docs = jnp.concatenate([docs, docs]).astype(bf16).reshape(1, LANES)
    sent = call(
        send_kernel, jax.ShapeDtypeStruct((planes, SENT, LANES), bf16), [VMEM] * 3, "send"
    )(by_rows, docs, out_weight.T)
    came = exchange(sent, PLANES)
    queries, keys = call(
        gather_kernel,
        [
            jax.ShapeDtypeStruct((ROWS + 16, LANES), bf16),
            jax.ShapeDtypeStruct((sources, GATHERED, LANES), bf16),
        ],
        [VMEM],
        "spread",
    )(came)
    keys = exchange(keys, KEY_AXES)
    queries = lax.all_gather(queries, QUERY_AXES)

    parts = call(
        attend_kernel,
        jax.ShapeDtypeStruct((spread, ROWS + 8, LANES), f32),
        [SMEM] + [VMEM] * 2,
        "attend",
        [pltpu.VMEM((sources, 2 * ROWS, LANES), f32)],
        4 * spread * ROWS * sources * ROWS * HEAD_DIM,
        2 << 20,
    )(place, queries, keys)
    parts = exchange(parts, QUERY_AXES)

    def from_y(block, k):
        return moved(block, lambda z, y, x, c: (z, (y - k) % 4, x, c))

    held = jax.ShapeDtypeStruct((sources, GATHERED - COLUMNS_AT, LANES), bf16)
    own = call(columns_kernel, held, [VMEM, pl.BlockSpec(memory_space=pl.ANY)], "columns")(
        keys, queries
    )
    other = moved(own, lambda z, y, x, c: (z ^ 2, y, x, c))
    next_own = from_y(own, 1)
    attended, own, other = call(
        combine_kernel,
        [jax.ShapeDtypeStruct((ROWS, HEAD_DIM), bf16), held, held],
        [VMEM] * 3,
        "combine",
    )(parts, own, other)
    weights = [own, next_own, from_y(next_own, 1), from_y(own, 3)]
    weights += [other] + [from_y(other, k) for k in (1, 2, 3)]

    back = exchange(attended.reshape(planes, EACH, HEAD_DIM), PLANES)
    everyone = exchange(jnp.broadcast_to(back[None], (groups, *back.shape)), HEAD_AXES)
    return call(
        product_kernel,
        jax.ShapeDtypeStruct(residual.shape, residual.dtype),
        [SMEM] + [VMEM] * 10,
        "product",
        (),
        2 * BLOCK * 2048 * 512,
        3 << 20,
    )(place, everyone, *weights, residual)


def solution(mesh):
    names, sizes = zip(*AXES)
    fine = Mesh(mesh.devices.reshape(sizes), names)
    seq, head = SEQ_AXES, HEAD_AXES
    placed = (P(seq, head), P(seq, head), P(seq, head), P(seq), P(head, seq), P(seq, head))
    return jax.shard_map(
        shards, mesh=fine, in_specs=placed, out_specs=P(seq, head), check_vma=False
    )
```

```python
import itertools

import jax
import jax.numpy as jnp
from jax import lax
from jax.experimental import pallas as pl
from jax.experimental.pallas import tpu as pltpu
from jax.sharding import Mesh, PartitionSpec as P

HEAD_DIM = 128
BLOCK = 64
LANES = 128
EACH = 8
ROWS = 128
COLUMNS = 32
HIDDEN = -1e30
LOWEST = -1e29
FACTOR = HEAD_DIM ** (-0.5) * 1.4426950408889634

AXES = (("zh", 8), ("zp", 2), ("z2", 2), ("y", 4), ("x", 4), ("c", 2))
SEQ_AXES = ("zh", "zp", "z2", "y")
HEAD_AXES = ("x", "c")
PLANES = ("zh", "zp")
KEY_AXES = ("z2", "x", "c")
QUERY_AXES = ("y",)

VMEM = pl.BlockSpec(memory_space=pltpu.VMEM)
SMEM = pl.BlockSpec(memory_space=pltpu.SMEM)


def exchange(tiles, axes):
    return lax.all_to_all(tiles, axes, split_axis=0, concat_axis=0, tiled=True)


def moved(block, where):
    sizes = (32, 4, 4, 2)
    places = itertools.product(*map(range, sizes))

    def flat(z, y, x, c):
        return ((z * 4 + y) * 4 + x) * 2 + c

    names = tuple(name for name, _ in AXES)
    return lax.ppermute(block, names, [(flat(*p), flat(*where(*p))) for p in places])


def transposed(row):
    return jnp.broadcast_to(row, (LANES, LANES)).T


def in_parts(value):
    parts = []
    for _ in range(3):
        part = value.astype(jnp.bfloat16).astype(jnp.float32)
        parts.append(part)
        value = value - part
    return parts


def call(kernel, out_shape, in_specs, name, scratch=(), flops=0, moved_bytes=1 << 20):
    many = isinstance(out_shape, (list, tuple))
    return pl.pallas_call(
        kernel,
        out_shape=out_shape,
        in_specs=in_specs,
        out_specs=[VMEM] * len(out_shape) if many else VMEM,
        scratch_shapes=list(scratch),
        compiler_params=pltpu.CompilerParams(vmem_limit_bytes=24 << 20),
        cost_estimate=pl.CostEstimate(flops=flops, bytes_accessed=moved_bytes, transcendentals=0),
        name=name,
    )


WEIGHT_AT = 4 * EACH
SENT = WEIGHT_AT + COLUMNS


def send_kernel(rows_ref, extra_ref, out_ref):
    docs = extra_ref[COLUMNS : COLUMNS + 16, 0:LANES].astype(jnp.float32)[0:EACH]
    for group in range(rows_ref.shape[0]):
        for j in range(2):
            lanes = slice(j * LANES, (j + 1) * LANES)
            values = rows_ref[group, 2 * EACH : 3 * EACH, lanes].astype(jnp.float32)
            tile = out_ref.at[2 * group + j]
            tile[0 : 2 * EACH, :] = rows_ref[group, 0 : 2 * EACH, lanes]
            tile[2 * EACH : 4 * EACH, :] = jnp.concatenate([values, docs], axis=0).astype(
                jnp.bfloat16
            )
            tile[WEIGHT_AT:SENT, :] = extra_ref[0:COLUMNS, lanes]


DOCS_AT = 2 * ROWS
COLUMNS_AT = DOCS_AT + 16
GATHERED = COLUMNS_AT + 2 * COLUMNS


def gather_kernel(came_ref, query_ref, key_ref):
    planes = came_ref.shape[0]
    first = [came_ref[i, 0 : 2 * EACH, :].astype(jnp.float32) for i in range(planes)]
    second = [came_ref[i, 2 * EACH : 4 * EACH, :].astype(jnp.float32) for i in range(planes)]
    queries, keys = (
        jnp.concatenate([t[k * EACH : (k + 1) * EACH] for t in first], axis=0).astype(jnp.bfloat16)
        for k in range(2)
    )
    values = jnp.concatenate([t[0:EACH] for t in second], axis=0).astype(jnp.bfloat16)
    lane = lax.broadcasted_iota(jnp.int32, (EACH, LANES), 1)
    docs = jnp.zeros((EACH, LANES), jnp.float32)
    for i, tile in enumerate(second):
        docs = jnp.where(lane // EACH == i, pltpu.roll(tile[EACH:], EACH * i, 1), docs)
    docs = jnp.concatenate([docs, docs], axis=0).astype(jnp.bfloat16)
    query_ref[0:ROWS, :] = queries
    query_ref[ROWS : ROWS + 16, :] = docs
    for s in range(key_ref.shape[0]):
        key_ref[s, 0:ROWS, :] = keys
        key_ref[s, ROWS:DOCS_AT, :] = values
        key_ref[s, DOCS_AT:COLUMNS_AT, :] = docs
        for k in range(2):
            at = COLUMNS_AT + k * COLUMNS
            key_ref[s, at : at + COLUMNS, :] = came_ref[2 * (s % 8) + k, WEIGHT_AT:SENT, :]


def attend_kernel(place_ref, query_ref, key_ref, out_ref, score_ref):
    z2, y, x, c = (place_ref[k] for k in range(4))
    stripe = 2 * BLOCK * 4

    def positions(z2, y, x, c, dim):
        index = lax.broadcasted_iota(jnp.int32, (ROWS, LANES), dim)
        first = (z2 * 4 + y) * BLOCK + EACH * (2 * x + c)
        return first + (index >> 3) * stripe + (index & 7)

    sources = key_ref.shape[0]
    key_docs = [
        key_ref[s, DOCS_AT:COLUMNS_AT, :].astype(jnp.float32)[0:1] for s in range(sources)
    ]
    key_pos = [positions(s // 8, y, s % 8 // 2, s % 2, 1)[0:1] for s in range(sources)]
    for first in range(0, query_ref.shape[0], 2):
        pair = (first, first + 1)
        queries = jnp.concatenate([query_ref[r, 0:ROWS, :] for r in pair], axis=0)
        query_docs = jnp.concatenate(
            [
                transposed(query_ref[r, ROWS : ROWS + 16, :].astype(jnp.float32)[0:1])
                for r in pair
            ],
            axis=0,
        )
        query_pos = jnp.concatenate([positions(z2, r, x, c, 0) for r in pair], axis=0)
        shape = query_pos.shape
        highest = jnp.full(shape, HIDDEN, jnp.float32)
        for s in range(sources):
            scores = lax.dot_general(
                queries,
                key_ref[s, 0:ROWS, :],
                (((1,), (1,)), ((), ())),
                preferred_element_type=jnp.float32,
            )
            visible = (key_pos[s] <= query_pos) & (key_docs[s] == query_docs)
            scores = jnp.where(visible, scores, HIDDEN)
            score_ref[s] = scores
            highest = jnp.maximum(highest, scores)
        row_max = jnp.maximum(jnp.max(highest, axis=1, keepdims=True), LOWEST)
        row_max = jnp.broadcast_to(row_max, shape)
        total = jnp.zeros(shape, jnp.float32)
        mixed = jnp.zeros(shape, jnp.float32)
        for s in range(0, sources, 2):
            weights, values = [], []
            for k in (s, s + 1):
                weight = jnp.exp2((score_ref[k] - row_max) * FACTOR)
                total = total + weight
                weights.append(weight.astype(jnp.bfloat16))
                values.append(key_ref[k, ROWS:DOCS_AT, :])
            mixed = mixed + jnp.dot(
                jnp.concatenate(weights, axis=1),
                jnp.concatenate(values, axis=0),
                preferred_element_type=jnp.float32,
            )
        row_sum = jnp.broadcast_to(jnp.sum(total, axis=1, keepdims=True), shape)
        means = jnp.where(row_sum > 0.0, mixed / row_sum, 0.0).astype(jnp.bfloat16)
        for k, r in enumerate(pair):
            rows = slice(k * ROWS, (k + 1) * ROWS)
            out_ref[r, 0:ROWS, :] = means[rows]
            stats = in_parts(row_max[rows].T[0:1]) + in_parts(row_sum[rows].T[0:1])
            stats = jnp.concatenate(stats + [jnp.zeros((10, LANES), jnp.float32)], axis=0)
            out_ref[r, ROWS : ROWS + 16, :] = stats.astype(jnp.bfloat16)


def columns_kernel(key_ref, after_ref, out_ref):
    out_ref[...] = key_ref[:, COLUMNS_AT:GATHERED, :]


def combine_kernel(part_ref, own_ref, other_ref, out_ref, same_own_ref, same_other_ref):
    same_own_ref[...] = own_ref[...]
    same_other_ref[...] = other_ref[...]
    parts = part_ref.shape[0]
    stats = [part_ref[r, ROWS : ROWS + 16, :].astype(jnp.float32) for r in range(parts)]
    maxima = [t[0:1] + t[1:2] + t[2:3] for t in stats]
    sums = [t[3:4] + t[4:5] + t[5:6] for t in stats]
    row_max = maxima[0]
    for m in maxima[1:]:
        row_max = jnp.maximum(row_max, m)
    scales = [jnp.exp2((m - row_max) * FACTOR) for m in maxima]
    scales = [scale * s for scale, s in zip(scales, sums)]
    row_sum = sum(scales)
    mixed = jnp.zeros((ROWS, HEAD_DIM), jnp.float32)
    for r in range(parts):
        mean = part_ref[r, 0:ROWS, :].astype(jnp.float32)
        mixed = mixed + mean * transposed(scales[r] / row_sum)
    out_ref[...] = mixed.astype(out_ref.dtype)


def product_kernel(place_ref, attended_ref, *refs):
    weights, (residual_ref, out_ref) = refs[:8], refs[8:]
    y, zp = place_ref[1], place_ref[4]
    groups = attended_ref.shape[0]
    total = jnp.zeros(out_ref.shape, jnp.float32)
    for p in range(groups):
        heads = [
            attended_ref[:, 2 * p + (zp ^ j)].astype(jnp.float32).reshape(BLOCK, HEAD_DIM)
            for j in range(2)
        ]
        left = jnp.concatenate(heads, axis=1).astype(jnp.bfloat16)
        blocks = []
        for k in range(2):
            rows = slice(k * COLUMNS, (k + 1) * COLUMNS)
            for z2 in range(2):
                for own, other in zip(weights[:4], weights[4:]):
                    halves = [w[z2 * groups + p, rows, :] for w in (own, other)]
                    blocks.append(jnp.concatenate(halves, axis=1))
        total = total + lax.dot_general(
            left,
            jnp.concatenate(blocks, axis=0),
            (((1,), (1,)), ((), ())),
            preferred_element_type=jnp.float32,
        )
    for zl in range(4):
        columns = slice(zl * LANES, (zl + 1) * LANES)
        summed = pltpu.roll(total[:, columns], y * COLUMNS, 1)
        out_ref[:, columns] = (residual_ref[:, columns].astype(jnp.float32) + summed).astype(
            out_ref.dtype
        )


def shards(query, key_states, value_states, doc_ids, out_weight, residual):
    groups = lax.axis_size(HEAD_AXES)
    planes = lax.axis_size(PLANES)
    spread = lax.axis_size(QUERY_AXES)
    sources = lax.axis_size(KEY_AXES)
    bf16, f32 = jnp.bfloat16, jnp.float32
    index = [lax.axis_index(a) for a in ("z2", "y", "x", "c", "zp")]
    place = jnp.stack(index)

    cut = [a.reshape(groups, EACH, -1) for a in (query, key_states, value_states)]
    by_rows = exchange(jnp.concatenate(cut, axis=1), HEAD_AXES)
    first = (2 * lax.axis_index("x") + lax.axis_index("c")) * EACH
    docs = jnp.roll(doc_ids, -first)
    docs = jnp.tile(docs.astype(bf16), 2 * LANES // BLOCK)
    extra = jnp.concatenate([out_weight.T, jnp.broadcast_to(docs, (16, 2 * LANES))])
    sent = call(
        send_kernel, jax.ShapeDtypeStruct((planes, SENT, LANES), bf16), [VMEM] * 2, "send"
    )(by_rows, extra)
    came = exchange(sent, PLANES)
    queries, keys = call(
        gather_kernel,
        [
            jax.ShapeDtypeStruct((ROWS + 16, LANES), bf16),
            jax.ShapeDtypeStruct((sources, GATHERED, LANES), bf16),
        ],
        [VMEM],
        "spread",
    )(came)
    keys = exchange(keys, KEY_AXES)
    queries = lax.all_gather(queries, QUERY_AXES)

    parts = call(
        attend_kernel,
        jax.ShapeDtypeStruct((spread, ROWS + 16, LANES), bf16),
        [SMEM] + [VMEM] * 2,
        "attend",
        [pltpu.VMEM((sources, 2 * ROWS, LANES), f32)],
        4 * spread * ROWS * sources * ROWS * HEAD_DIM,
        2 << 20,
    )(place, queries, keys)
    parts = exchange(parts, QUERY_AXES)

    def from_y(block, k):
        return moved(block, lambda z, y, x, c: (z, (y - k) % 4, x, c))

    held = jax.ShapeDtypeStruct((sources, GATHERED - COLUMNS_AT, LANES), bf16)
    own = call(columns_kernel, held, [VMEM, pl.BlockSpec(memory_space=pl.ANY)], "columns")(
        keys, queries
    )
    other = moved(own, lambda z, y, x, c: (z ^ 2, y, x, c))
    next_own = from_y(own, 1)
    attended, own, other = call(
        combine_kernel,
        [jax.ShapeDtypeStruct((ROWS, HEAD_DIM), bf16), held, held],
        [VMEM] * 3,
        "combine",
    )(parts, own, other)
    weights = [own, next_own, from_y(next_own, 1), from_y(own, 3)]
    weights += [other] + [from_y(other, k) for k in (1, 2, 3)]

    back = exchange(attended.reshape(planes, EACH, HEAD_DIM), PLANES)
    everyone = exchange(jnp.broadcast_to(back[None], (groups, *back.shape)), HEAD_AXES)
    return call(
        product_kernel,
        jax.ShapeDtypeStruct(residual.shape, residual.dtype),
        [SMEM] + [VMEM] * 10,
        "product",
        (),
        2 * BLOCK * 2048 * 512,
        3 << 20,
    )(place, everyone, *weights, residual)


def solution(mesh):
    names, sizes = zip(*AXES)
    fine = Mesh(mesh.devices.reshape(sizes), names)
    seq, head = SEQ_AXES, HEAD_AXES
    placed = (P(seq, head), P(seq, head), P(seq, head), P(seq), P(head, seq), P(seq, head))
    return jax.shard_map(
        shards, mesh=fine, in_specs=placed, out_specs=P(seq, head), check_vma=False
    )
```

```python
import itertools

import jax
import jax.numpy as jnp
from jax import lax
from jax.experimental import pallas as pl
from jax.experimental.pallas import tpu as pltpu
from jax.sharding import Mesh, PartitionSpec as P

HEAD_DIM = 128
BLOCK = 64
LANES = 128
EACH = 8
ROWS = 128
COLUMNS = 32
HIDDEN = -1e30
LOWEST = -1e29
FACTOR = HEAD_DIM ** (-0.5) * 1.4426950408889634

AXES = (("zh", 8), ("zp", 2), ("z2", 2), ("y", 4), ("x", 4), ("c", 2))
SEQ_AXES = ("zh", "zp", "z2", "y")
HEAD_AXES = ("x", "c")
PLANES = ("zh", "zp")
KEY_AXES = ("z2", "x", "c")
QUERY_AXES = ("y",)

VMEM = pl.BlockSpec(memory_space=pltpu.VMEM)
SMEM = pl.BlockSpec(memory_space=pltpu.SMEM)


def exchange(tiles, axes):
    return lax.all_to_all(tiles, axes, split_axis=0, concat_axis=0, tiled=True)


def moved(block, where):
    sizes = (32, 4, 4, 2)
    places = itertools.product(*map(range, sizes))

    def flat(z, y, x, c):
        return ((z * 4 + y) * 4 + x) * 2 + c

    names = tuple(name for name, _ in AXES)
    return lax.ppermute(block, names, [(flat(*p), flat(*where(*p))) for p in places])


def transposed(row):
    return jnp.broadcast_to(row, (LANES, LANES)).T


def in_parts(value):
    parts = []
    for _ in range(3):
        part = value.astype(jnp.bfloat16).astype(jnp.float32)
        parts.append(part)
        value = value - part
    return parts


def call(kernel, out_shape, in_specs, name, scratch=(), flops=0, moved_bytes=1 << 20):
    many = isinstance(out_shape, (list, tuple))
    return pl.pallas_call(
        kernel,
        out_shape=out_shape,
        in_specs=in_specs,
        out_specs=[VMEM] * len(out_shape) if many else VMEM,
        scratch_shapes=list(scratch),
        compiler_params=pltpu.CompilerParams(vmem_limit_bytes=24 << 20),
        cost_estimate=pl.CostEstimate(flops=flops, bytes_accessed=moved_bytes, transcendentals=0),
        name=name,
    )


WEIGHT_AT = 4 * EACH
SENT = WEIGHT_AT + COLUMNS


def send_kernel(rows_ref, extra_ref, out_ref):
    docs = extra_ref[COLUMNS : COLUMNS + 16, 0:LANES].astype(jnp.float32)[0:EACH]
    for group in range(rows_ref.shape[0]):
        for j in range(2):
            lanes = slice(j * LANES, (j + 1) * LANES)
            values = rows_ref[group, 2 * EACH : 3 * EACH, lanes].astype(jnp.float32)
            tile = out_ref.at[2 * group + j]
            tile[0 : 2 * EACH, :] = rows_ref[group, 0 : 2 * EACH, lanes]
            tile[2 * EACH : 4 * EACH, :] = jnp.concatenate([values, docs], axis=0).astype(
                jnp.bfloat16
            )
            tile[WEIGHT_AT:SENT, :] = extra_ref[0:COLUMNS, lanes]


DOCS_AT = ROWS
COLUMNS_AT = DOCS_AT + 16
GATHERED = COLUMNS_AT + 2 * COLUMNS


def gather_kernel(came_ref, query_ref, key_ref):
    planes = came_ref.shape[0]
    first = [came_ref[i, 0 : 2 * EACH, :].astype(jnp.float32) for i in range(planes)]
    second = [came_ref[i, 2 * EACH : 4 * EACH, :].astype(jnp.float32) for i in range(planes)]
    queries, keys = (
        jnp.concatenate([t[k * EACH : (k + 1) * EACH] for t in first], axis=0).astype(jnp.bfloat16)
        for k in range(2)
    )
    values = jnp.concatenate([t[0:EACH] for t in second], axis=0).astype(jnp.bfloat16)
    lane = lax.broadcasted_iota(jnp.int32, (EACH, LANES), 1)
    docs = jnp.zeros((EACH, LANES), jnp.float32)
    for i, tile in enumerate(second):
        docs = jnp.where(lane // EACH == i, pltpu.roll(tile[EACH:], EACH * i, 1), docs)
    docs = jnp.concatenate([docs, docs], axis=0).astype(jnp.bfloat16)
    query_ref[0:ROWS, :] = queries
    query_ref[ROWS : ROWS + 16, :] = docs
    for s in range(key_ref.shape[0]):
        key_ref[s, 0:ROWS, :] = (keys, values)[s % 2]
        key_ref[s, DOCS_AT:COLUMNS_AT, :] = docs
        for k in range(2):
            at = COLUMNS_AT + k * COLUMNS
            key_ref[s, at : at + COLUMNS, :] = came_ref[2 * (s % 8) + k, WEIGHT_AT:SENT, :]


def attend_kernel(
    place_ref, query_ref, key_ref, swapped_ref, out_ref, score_ref, keys_ref, values_ref
):
    z2, y, x, c = (place_ref[k] for k in range(4))

    @pl.when(c == 0)
    def _():
        keys_ref[...] = key_ref[:, 0:ROWS, :]
        values_ref[...] = swapped_ref[...]

    @pl.when(c != 0)
    def _():
        keys_ref[...] = swapped_ref[...]
        values_ref[...] = key_ref[:, 0:ROWS, :]

    stripe = 2 * BLOCK * 4

    def positions(z2, y, x, c, dim):
        index = lax.broadcasted_iota(jnp.int32, (ROWS, LANES), dim)
        first = (z2 * 4 + y) * BLOCK + EACH * (2 * x + c)
        return first + (index >> 3) * stripe + (index & 7)

    sources = key_ref.shape[0]
    key_docs = [
        key_ref[s, DOCS_AT:COLUMNS_AT, :].astype(jnp.float32)[0:1] for s in range(sources)
    ]
    key_pos = [positions(s // 8, y, s % 8 // 2, s % 2, 1)[0:1] for s in range(sources)]
    for first in range(0, query_ref.shape[0], 2):
        pair = (first, first + 1)
        queries = jnp.concatenate([query_ref[r, 0:ROWS, :] for r in pair], axis=0)
        query_docs = jnp.concatenate(
            [
                transposed(query_ref[r, ROWS : ROWS + 16, :].astype(jnp.float32)[0:1])
                for r in pair
            ],
            axis=0,
        )
        query_pos = jnp.concatenate([positions(z2, r, x, c, 0) for r in pair], axis=0)
        shape = query_pos.shape
        highest = jnp.full(shape, HIDDEN, jnp.float32)
        for s in range(sources):
            scores = lax.dot_general(
                queries,
                keys_ref[s],
                (((1,), (1,)), ((), ())),
                preferred_element_type=jnp.float32,
            )
            visible = (key_pos[s] <= query_pos) & (key_docs[s] == query_docs)
            scores = jnp.where(visible, scores, HIDDEN)
            score_ref[s] = scores
            highest = jnp.maximum(highest, scores)
        row_max = jnp.maximum(jnp.max(highest, axis=1, keepdims=True), LOWEST)
        row_max = jnp.broadcast_to(row_max, shape)
        total = jnp.zeros(shape, jnp.float32)
        mixed = jnp.zeros(shape, jnp.float32)
        for s in range(0, sources, 2):
            weights, values = [], []
            for k in (s, s + 1):
                weight = jnp.exp2((score_ref[k] - row_max) * FACTOR)
                total = total + weight
                weights.append(weight.astype(jnp.bfloat16))
                values.append(values_ref[k])
            mixed = mixed + jnp.dot(
                jnp.concatenate(weights, axis=1),
                jnp.concatenate(values, axis=0),
                preferred_element_type=jnp.float32,
            )
        row_sum = jnp.broadcast_to(jnp.sum(total, axis=1, keepdims=True), shape)
        means = jnp.where(row_sum > 0.0, mixed / row_sum, 0.0).astype(jnp.bfloat16)
        for k, r in enumerate(pair):
            rows = slice(k * ROWS, (k + 1) * ROWS)
            out_ref[r, 0:ROWS, :] = means[rows]
            stats = in_parts(row_max[rows].T[0:1]) + in_parts(row_sum[rows].T[0:1])
            stats = jnp.concatenate(stats + [jnp.zeros((10, LANES), jnp.float32)], axis=0)
            out_ref[r, ROWS : ROWS + 16, :] = stats.astype(jnp.bfloat16)


def columns_kernel(key_ref, after_ref, out_ref, half_ref):
    out_ref[...] = key_ref[:, COLUMNS_AT:GATHERED, :]
    half_ref[...] = key_ref[:, 0:ROWS, :]


def combine_kernel(part_ref, own_ref, other_ref, out_ref, same_own_ref, same_other_ref):
    same_own_ref[...] = own_ref[...]
    same_other_ref[...] = other_ref[...]
    parts = part_ref.shape[0]
    stats = [part_ref[r, ROWS : ROWS + 16, :].astype(jnp.float32) for r in range(parts)]
    maxima = [t[0:1] + t[1:2] + t[2:3] for t in stats]
    sums = [t[3:4] + t[4:5] + t[5:6] for t in stats]
    row_max = maxima[0]
    for m in maxima[1:]:
        row_max = jnp.maximum(row_max, m)
    scales = [jnp.exp2((m - row_max) * FACTOR) for m in maxima]
    scales = [scale * s for scale, s in zip(scales, sums)]
    row_sum = sum(scales)
    mixed = jnp.zeros((ROWS, HEAD_DIM), jnp.float32)
    for r in range(parts):
        mean = part_ref[r, 0:ROWS, :].astype(jnp.float32)
        mixed = mixed + mean * transposed(scales[r] / row_sum)
    out_ref[...] = mixed.astype(out_ref.dtype)


def product_kernel(place_ref, attended_ref, *refs):
    weights, (residual_ref, out_ref) = refs[:8], refs[8:]
    y, zp = place_ref[1], place_ref[4]
    groups = attended_ref.shape[0]
    total = jnp.zeros(out_ref.shape, jnp.float32)
    for p in range(groups):
        heads = [
            attended_ref[:, 2 * p + (zp ^ j)].astype(jnp.float32).reshape(BLOCK, HEAD_DIM)
            for j in range(2)
        ]
        left = jnp.concatenate(heads, axis=1).astype(jnp.bfloat16)
        blocks = []
        for k in range(2):
            rows = slice(k * COLUMNS, (k + 1) * COLUMNS)
            for z2 in range(2):
                for own, other in zip(weights[:4], weights[4:]):
                    halves = [w[z2 * groups + p, rows, :] for w in (own, other)]
                    blocks.append(jnp.concatenate(halves, axis=1))
        total = total + lax.dot_general(
            left,
            jnp.concatenate(blocks, axis=0),
            (((1,), (1,)), ((), ())),
            preferred_element_type=jnp.float32,
        )
    for zl in range(4):
        columns = slice(zl * LANES, (zl + 1) * LANES)
        summed = pltpu.roll(total[:, columns], y * COLUMNS, 1)
        out_ref[:, columns] = (residual_ref[:, columns].astype(jnp.float32) + summed).astype(
            out_ref.dtype
        )


def shards(query, key_states, value_states, doc_ids, out_weight, residual):
    groups = lax.axis_size(HEAD_AXES)
    planes = lax.axis_size(PLANES)
    spread = lax.axis_size(QUERY_AXES)
    sources = lax.axis_size(KEY_AXES)
    bf16, f32 = jnp.bfloat16, jnp.float32
    index = [lax.axis_index(a) for a in ("z2", "y", "x", "c", "zp")]
    place = jnp.stack(index)

    cut = [a.reshape(groups, EACH, -1) for a in (query, key_states, value_states)]
    by_rows = exchange(jnp.concatenate(cut, axis=1), HEAD_AXES)
    first = (2 * lax.axis_index("x") + lax.axis_index("c")) * EACH
    docs = jnp.roll(doc_ids, -first)
    docs = jnp.tile(docs.astype(bf16), 2 * LANES // BLOCK)
    extra = jnp.concatenate([out_weight.T, jnp.broadcast_to(docs, (16, 2 * LANES))])
    sent = call(
        send_kernel, jax.ShapeDtypeStruct((planes, SENT, LANES), bf16), [VMEM] * 2, "send"
    )(by_rows, extra)
    came = exchange(sent, PLANES)
    queries, keys = call(
        gather_kernel,
        [
            jax.ShapeDtypeStruct((ROWS + 16, LANES), bf16),
            jax.ShapeDtypeStruct((sources, GATHERED, LANES), bf16),
        ],
        [VMEM],
        "spread",
    )(came)
    keys = exchange(keys, KEY_AXES)
    queries = lax.all_gather(queries, QUERY_AXES)

    held = jax.ShapeDtypeStruct((sources, GATHERED - COLUMNS_AT, LANES), bf16)
    half = jax.ShapeDtypeStruct((sources, ROWS, LANES), bf16)
    own, half = call(
        columns_kernel, [held, half], [VMEM, pl.BlockSpec(memory_space=pl.ANY)], "columns"
    )(keys, queries)
    swapped = moved(half, lambda z, y, x, c: (z, y, x, 1 - c))

    parts = call(
        attend_kernel,
        jax.ShapeDtypeStruct((spread, ROWS + 16, LANES), bf16),
        [SMEM] + [VMEM] * 3,
        "attend",
        [
            pltpu.VMEM((sources, 2 * ROWS, LANES), f32),
            pltpu.VMEM((sources, ROWS, LANES), bf16),
            pltpu.VMEM((sources, ROWS, LANES), bf16),
        ],
        4 * spread * ROWS * sources * ROWS * HEAD_DIM,
        2 << 20,
    )(place, queries, keys, swapped)
    parts = exchange(parts, QUERY_AXES)

    def from_y(block, k):
        return moved(block, lambda z, y, x, c: (z, (y - k) % 4, x, c))

    other = moved(own, lambda z, y, x, c: (z ^ 2, y, x, c))
    next_own = from_y(own, 1)
    attended, own, other = call(
        combine_kernel,
        [jax.ShapeDtypeStruct((ROWS, HEAD_DIM), bf16), held, held],
        [VMEM] * 3,
        "combine",
    )(parts, own, other)
    weights = [own, next_own, from_y(next_own, 1), from_y(own, 3)]
    weights += [other] + [from_y(other, k) for k in (1, 2, 3)]

    back = exchange(attended.reshape(planes, EACH, HEAD_DIM), PLANES)
    everyone = exchange(jnp.broadcast_to(back[None], (groups, *back.shape)), HEAD_AXES)
    return call(
        product_kernel,
        jax.ShapeDtypeStruct(residual.shape, residual.dtype),
        [SMEM] + [VMEM] * 10,
        "product",
        (),
        2 * BLOCK * 2048 * 512,
        3 << 20,
    )(place, everyone, *weights, residual)


def solution(mesh):
    names, sizes = zip(*AXES)
    fine = Mesh(mesh.devices.reshape(sizes), names)
    seq, head = SEQ_AXES, HEAD_AXES
    placed = (P(seq, head), P(seq, head), P(seq, head), P(seq), P(head, seq), P(seq, head))
    return jax.shard_map(
        shards, mesh=fine, in_specs=placed, out_specs=P(seq, head), check_vma=False
    )
```

```python
import itertools

import jax
import jax.numpy as jnp
from jax import lax
from jax.experimental import pallas as pl
from jax.experimental.pallas import tpu as pltpu
from jax.sharding import Mesh, PartitionSpec as P

HEAD_DIM = 128
BLOCK = 64
LANES = 128
EACH = 8
ROWS = 128
COLUMNS = 32
HIDDEN = -1e30
LOWEST = -1e29
FACTOR = HEAD_DIM ** (-0.5) * 1.4426950408889634

AXES = (("zh", 8), ("zp", 2), ("z2", 2), ("y", 4), ("x", 4), ("c", 2))
SEQ_AXES = ("zh", "zp", "z2", "y")
HEAD_AXES = ("x", "c")
PLANES = ("zh", "zp")
KEY_AXES = ("z2", "x", "c")
QUERY_AXES = ("y",)

VMEM = pl.BlockSpec(memory_space=pltpu.VMEM)
SMEM = pl.BlockSpec(memory_space=pltpu.SMEM)


def exchange(tiles, axes):
    return lax.all_to_all(tiles, axes, split_axis=0, concat_axis=0, tiled=True)


def moved(block, where):
    sizes = (32, 4, 4, 2)
    places = itertools.product(*map(range, sizes))

    def flat(z, y, x, c):
        return ((z * 4 + y) * 4 + x) * 2 + c

    names = tuple(name for name, _ in AXES)
    return lax.ppermute(block, names, [(flat(*p), flat(*where(*p))) for p in places])


def transposed(row):
    return jnp.broadcast_to(row, (LANES, LANES)).T


def in_parts(value):
    parts = []
    for _ in range(3):
        part = value.astype(jnp.bfloat16).astype(jnp.float32)
        parts.append(part)
        value = value - part
    return parts


def call(kernel, out_shape, in_specs, name, scratch=(), flops=0, moved_bytes=1 << 20):
    many = isinstance(out_shape, (list, tuple))
    return pl.pallas_call(
        kernel,
        out_shape=out_shape,
        in_specs=in_specs,
        out_specs=[VMEM] * len(out_shape) if many else VMEM,
        scratch_shapes=list(scratch),
        compiler_params=pltpu.CompilerParams(vmem_limit_bytes=24 << 20),
        cost_estimate=pl.CostEstimate(flops=flops, bytes_accessed=moved_bytes, transcendentals=0),
        name=name,
    )


WEIGHT_AT = 4 * EACH
SENT = WEIGHT_AT + COLUMNS


def send_kernel(rows_ref, extra_ref, out_ref):
    docs = extra_ref[COLUMNS : COLUMNS + 16, 0:LANES].astype(jnp.float32)[0:EACH]
    for group in range(rows_ref.shape[0]):
        for j in range(2):
            lanes = slice(j * LANES, (j + 1) * LANES)
            values = rows_ref[group, 2 * EACH : 3 * EACH, lanes].astype(jnp.float32)
            tile = out_ref.at[2 * group + j]
            tile[0 : 2 * EACH, :] = rows_ref[group, 0 : 2 * EACH, lanes]
            tile[2 * EACH : 4 * EACH, :] = jnp.concatenate([values, docs], axis=0).astype(
                jnp.bfloat16
            )
            tile[WEIGHT_AT:SENT, :] = extra_ref[0:COLUMNS, lanes]


DOCS_AT = ROWS
COLUMNS_AT = DOCS_AT + 16
GATHERED = COLUMNS_AT + 2 * COLUMNS


def gather_kernel(came_ref, query_ref, key_ref):
    planes = came_ref.shape[0]
    first = [came_ref[i, 0 : 2 * EACH, :].astype(jnp.float32) for i in range(planes)]
    second = [came_ref[i, 2 * EACH : 4 * EACH, :].astype(jnp.float32) for i in range(planes)]
    queries, keys = (
        jnp.concatenate([t[k * EACH : (k + 1) * EACH] for t in first], axis=0).astype(jnp.bfloat16)
        for k in range(2)
    )
    values = jnp.concatenate([t[0:EACH] for t in second], axis=0).astype(jnp.bfloat16)
    lane = lax.broadcasted_iota(jnp.int32, (EACH, LANES), 1)
    docs = jnp.zeros((EACH, LANES), jnp.float32)
    for i, tile in enumerate(second):
        docs = jnp.where(lane // EACH == i, pltpu.roll(tile[EACH:], EACH * i, 1), docs)
    docs = jnp.concatenate([docs, docs], axis=0).astype(jnp.bfloat16)
    query_ref[0:ROWS, :] = queries
    query_ref[ROWS : ROWS + 16, :] = docs
    for s in range(key_ref.shape[0]):
        key_ref[s, 0:ROWS, :] = (keys, values)[s % 2]
        key_ref[s, DOCS_AT:COLUMNS_AT, :] = docs
        for k in range(2):
            at = COLUMNS_AT + k * COLUMNS
            key_ref[s, at : at + COLUMNS, :] = came_ref[2 * (s % 8) + k, WEIGHT_AT:SENT, :]


def attend_kernel(
    place_ref, query_ref, key_ref, swapped_ref, out_ref, score_ref, keys_ref, values_ref
):
    z2, y, x, c = (place_ref[k] for k in range(4))

    @pl.when(c == 0)
    def _():
        keys_ref[...] = key_ref[:, 0:ROWS, :]
        values_ref[...] = swapped_ref[...]

    @pl.when(c != 0)
    def _():
        keys_ref[...] = swapped_ref[...]
        values_ref[...] = key_ref[:, 0:ROWS, :]

    stripe = 2 * BLOCK * 4

    def positions(z2, y, x, c, dim):
        index = lax.broadcasted_iota(jnp.int32, (ROWS, LANES), dim)
        first = (z2 * 4 + y) * BLOCK + EACH * (2 * x + c)
        return first + (index >> 3) * stripe + (index & 7)

    sources = key_ref.shape[0]
    key_docs = [
        key_ref[s, DOCS_AT:COLUMNS_AT, :].astype(jnp.float32)[0:1] for s in range(sources)
    ]
    key_pos = [positions(s // 8, y, s % 8 // 2, s % 2, 1)[0:1] for s in range(sources)]
    for first in range(0, query_ref.shape[0], 2):
        pair = (first, first + 1)
        queries = jnp.concatenate([query_ref[r, 0:ROWS, :] for r in pair], axis=0)
        query_docs = jnp.concatenate(
            [
                transposed(query_ref[r, ROWS : ROWS + 16, :].astype(jnp.float32)[0:1])
                for r in pair
            ],
            axis=0,
        )
        query_pos = jnp.concatenate([positions(z2, r, x, c, 0) for r in pair], axis=0)
        shape = query_pos.shape
        highest = jnp.full(shape, HIDDEN, jnp.float32)
        for s in range(sources):
            scores = lax.dot_general(
                queries,
                keys_ref[s],
                (((1,), (1,)), ((), ())),
                preferred_element_type=jnp.float32,
            )
            visible = (key_pos[s] <= query_pos) & (key_docs[s] == query_docs)
            scores = jnp.where(visible, scores, HIDDEN)
            score_ref[s] = scores
            highest = jnp.maximum(highest, scores)
        row_max = jnp.maximum(jnp.max(highest, axis=1, keepdims=True), LOWEST)
        row_max = jnp.broadcast_to(row_max, shape)
        total = jnp.zeros(shape, jnp.float32)
        mixed = jnp.zeros(shape, jnp.float32)
        for s in range(0, sources, 2):
            weights, values = [], []
            for k in (s, s + 1):
                weight = jnp.exp2((score_ref[k] - row_max) * FACTOR)
                total = total + weight
                weights.append(weight.astype(jnp.bfloat16))
                values.append(values_ref[k])
            mixed = mixed + jnp.dot(
                jnp.concatenate(weights, axis=1),
                jnp.concatenate(values, axis=0),
                preferred_element_type=jnp.float32,
            )
        row_sum = jnp.broadcast_to(jnp.sum(total, axis=1, keepdims=True), shape)
        means = jnp.where(row_sum > 0.0, mixed / row_sum, 0.0).astype(jnp.bfloat16)
        for k, r in enumerate(pair):
            rows = slice(k * ROWS, (k + 1) * ROWS)
            out_ref[r, 0:ROWS, :] = means[rows]
            stats = in_parts(row_max[rows].T[0:1]) + in_parts(row_sum[rows].T[0:1])
            stats = jnp.concatenate(stats + [jnp.zeros((10, LANES), jnp.float32)], axis=0)
            out_ref[r, ROWS : ROWS + 16, :] = stats.astype(jnp.bfloat16)


def columns_kernel(key_ref, after_ref, out_ref, half_ref):
    out_ref[...] = key_ref[:, COLUMNS_AT:GATHERED, :]
    half_ref[...] = key_ref[:, 0:ROWS, :]


def after_kernel(block_ref, after_ref, out_ref):
    out_ref[...] = block_ref[...]


def combine_kernel(part_ref, own_ref, out_ref, same_own_ref):
    same_own_ref[...] = own_ref[...]
    parts = part_ref.shape[0]
    stats = [part_ref[r, ROWS : ROWS + 16, :].astype(jnp.float32) for r in range(parts)]
    maxima = [t[0:1] + t[1:2] + t[2:3] for t in stats]
    sums = [t[3:4] + t[4:5] + t[5:6] for t in stats]
    row_max = maxima[0]
    for m in maxima[1:]:
        row_max = jnp.maximum(row_max, m)
    scales = [jnp.exp2((m - row_max) * FACTOR) for m in maxima]
    scales = [scale * s for scale, s in zip(scales, sums)]
    row_sum = sum(scales)
    mixed = jnp.zeros((ROWS, HEAD_DIM), jnp.float32)
    for r in range(parts):
        mean = part_ref[r, 0:ROWS, :].astype(jnp.float32)
        mixed = mixed + mean * transposed(scales[r] / row_sum)
    out_ref[...] = mixed.astype(out_ref.dtype)


def product_kernel(place_ref, attended_ref, *refs):
    weights, (residual_ref, out_ref) = refs[:8], refs[8:]
    y, zp = place_ref[1], place_ref[4]
    groups = attended_ref.shape[0]
    total = jnp.zeros(out_ref.shape, jnp.float32)
    for p in range(groups):
        heads = [
            attended_ref[:, 2 * p + (zp ^ j)].astype(jnp.float32).reshape(BLOCK, HEAD_DIM)
            for j in range(2)
        ]
        left = jnp.concatenate(heads, axis=1).astype(jnp.bfloat16)
        blocks = []
        for k in range(2):
            rows = slice(k * COLUMNS, (k + 1) * COLUMNS)
            for z2 in range(2):
                for own, other in zip(weights[:4], weights[4:]):
                    halves = [w[z2 * groups + p, rows, :] for w in (own, other)]
                    blocks.append(jnp.concatenate(halves, axis=1))
        total = total + lax.dot_general(
            left,
            jnp.concatenate(blocks, axis=0),
            (((1,), (1,)), ((), ())),
            preferred_element_type=jnp.float32,
        )
    for zl in range(4):
        columns = slice(zl * LANES, (zl + 1) * LANES)
        summed = pltpu.roll(total[:, columns], y * COLUMNS, 1)
        out_ref[:, columns] = (residual_ref[:, columns].astype(jnp.float32) + summed).astype(
            out_ref.dtype
        )


def shards(query, key_states, value_states, doc_ids, out_weight, residual):
    groups = lax.axis_size(HEAD_AXES)
    planes = lax.axis_size(PLANES)
    spread = lax.axis_size(QUERY_AXES)
    sources = lax.axis_size(KEY_AXES)
    bf16, f32 = jnp.bfloat16, jnp.float32
    index = [lax.axis_index(a) for a in ("z2", "y", "x", "c", "zp")]
    place = jnp.stack(index)

    cut = [a.reshape(groups, EACH, -1) for a in (query, key_states, value_states)]
    by_rows = exchange(jnp.concatenate(cut, axis=1), HEAD_AXES)
    first = (2 * lax.axis_index("x") + lax.axis_index("c")) * EACH
    docs = jnp.roll(doc_ids, -first)
    docs = jnp.tile(docs.astype(bf16), 2 * LANES // BLOCK)
    extra = jnp.concatenate([out_weight.T, jnp.broadcast_to(docs, (16, 2 * LANES))])
    sent = call(
        send_kernel, jax.ShapeDtypeStruct((planes, SENT, LANES), bf16), [VMEM] * 2, "send"
    )(by_rows, extra)
    came = exchange(sent, PLANES)
    queries, keys = call(
        gather_kernel,
        [
            jax.ShapeDtypeStruct((ROWS + 16, LANES), bf16),
            jax.ShapeDtypeStruct((sources, GATHERED, LANES), bf16),
        ],
        [VMEM],
        "spread",
    )(came)
    keys = exchange(keys, KEY_AXES)
    queries = lax.all_gather(queries, QUERY_AXES)

    held = jax.ShapeDtypeStruct((sources, GATHERED - COLUMNS_AT, LANES), bf16)
    half = jax.ShapeDtypeStruct((sources, ROWS, LANES), bf16)
    own, half = call(
        columns_kernel, [held, half], [VMEM, pl.BlockSpec(memory_space=pl.ANY)], "columns"
    )(keys, queries)
    swapped = moved(half, lambda z, y, x, c: (z, y, x, 1 - c))

    parts = call(
        attend_kernel,
        jax.ShapeDtypeStruct((spread, ROWS + 16, LANES), bf16),
        [SMEM] + [VMEM] * 3,
        "attend",
        [
            pltpu.VMEM((sources, 2 * ROWS, LANES), f32),
            pltpu.VMEM((sources, ROWS, LANES), bf16),
            pltpu.VMEM((sources, ROWS, LANES), bf16),
        ],
        4 * spread * ROWS * sources * ROWS * HEAD_DIM,
        2 << 20,
    )(place, queries, keys, swapped)
    parts = exchange(parts, QUERY_AXES)

    def from_y(block, k):
        return moved(block, lambda z, y, x, c: (z, (y - k) % 4, x, c))

    other = moved(own, lambda z, y, x, c: (z ^ 2, y, x, c))
    next_own = from_y(own, 1)
    attended, own = call(
        combine_kernel,
        [jax.ShapeDtypeStruct((ROWS, HEAD_DIM), bf16), held],
        [VMEM] * 2,
        "combine",
    )(parts, own)
    other = call(after_kernel, held, [VMEM, pl.BlockSpec(memory_space=pl.ANY)], "after")(
        other, attended
    )
    weights = [own, next_own, from_y(next_own, 1), from_y(own, 3)]
    weights += [other] + [from_y(other, k) for k in (1, 2, 3)]

    back = exchange(attended.reshape(planes, EACH, HEAD_DIM), PLANES)
    everyone = exchange(jnp.broadcast_to(back[None], (groups, *back.shape)), HEAD_AXES)
    return call(
        product_kernel,
        jax.ShapeDtypeStruct(residual.shape, residual.dtype),
        [SMEM] + [VMEM] * 10,
        "product",
        (),
        2 * BLOCK * 2048 * 512,
        3 << 20,
    )(place, everyone, *weights, residual)


def solution(mesh):
    names, sizes = zip(*AXES)
    fine = Mesh(mesh.devices.reshape(sizes), names)
    seq, head = SEQ_AXES, HEAD_AXES
    placed = (P(seq, head), P(seq, head), P(seq, head), P(seq), P(head, seq), P(seq, head))
    return jax.shard_map(
        shards, mesh=fine, in_specs=placed, out_specs=P(seq, head), check_vma=False
    )
```

```python
import itertools

import jax
import jax.numpy as jnp
from jax import lax
from jax.experimental import pallas as pl
from jax.experimental.pallas import tpu as pltpu
from jax.sharding import Mesh, PartitionSpec as P

HEAD_DIM = 128
BLOCK = 64
LANES = 128
EACH = 8
ROWS = 128
COLUMNS = 32
HIDDEN = -1e30
LOWEST = -1e29
FACTOR = HEAD_DIM ** (-0.5) * 1.4426950408889634

AXES = (("zh", 8), ("zp", 2), ("z2", 2), ("y", 4), ("x", 4), ("c", 2))
SEQ_AXES = ("zh", "zp", "z2", "y")
HEAD_AXES = ("x", "c")
PLANES = ("zh", "zp")
KEY_AXES = ("z2", "x", "c")
QUERY_AXES = ("y",)

VMEM = pl.BlockSpec(memory_space=pltpu.VMEM)
SMEM = pl.BlockSpec(memory_space=pltpu.SMEM)


def exchange(tiles, axes):
    return lax.all_to_all(tiles, axes, split_axis=0, concat_axis=0, tiled=True)


def moved(block, where):
    sizes = (32, 4, 4, 2)
    places = itertools.product(*map(range, sizes))

    def flat(z, y, x, c):
        return ((z * 4 + y) * 4 + x) * 2 + c

    names = tuple(name for name, _ in AXES)
    return lax.ppermute(block, names, [(flat(*p), flat(*where(*p))) for p in places])


def transposed(row):
    return jnp.broadcast_to(row, (LANES, LANES)).T


def in_parts(value):
    parts = []
    for _ in range(3):
        part = value.astype(jnp.bfloat16).astype(jnp.float32)
        parts.append(part)
        value = value - part
    return parts


def call(kernel, out_shape, in_specs, name, scratch=(), flops=0, moved_bytes=1 << 20):
    many = isinstance(out_shape, (list, tuple))
    return pl.pallas_call(
        kernel,
        out_shape=out_shape,
        in_specs=in_specs,
        out_specs=[VMEM] * len(out_shape) if many else VMEM,
        scratch_shapes=list(scratch),
        compiler_params=pltpu.CompilerParams(vmem_limit_bytes=24 << 20),
        cost_estimate=pl.CostEstimate(flops=flops, bytes_accessed=moved_bytes, transcendentals=0),
        name=name,
    )


WEIGHT_AT = 4 * EACH
SENT = WEIGHT_AT + COLUMNS


def send_kernel(rows_ref, extra_ref, out_ref):
    docs = extra_ref[COLUMNS : COLUMNS + 16, 0:LANES].astype(jnp.float32)[0:EACH]
    for group in range(rows_ref.shape[0]):
        for j in range(2):
            lanes = slice(j * LANES, (j + 1) * LANES)
            values = rows_ref[group, 2 * EACH : 3 * EACH, lanes].astype(jnp.float32)
            tile = out_ref.at[2 * group + j]
            tile[0 : 2 * EACH, :] = rows_ref[group, 0 : 2 * EACH, lanes]
            tile[2 * EACH : 4 * EACH, :] = jnp.concatenate([values, docs], axis=0).astype(
                jnp.bfloat16
            )
            tile[WEIGHT_AT:SENT, :] = extra_ref[0:COLUMNS, lanes]


DOCS_AT = ROWS
COLUMNS_AT = DOCS_AT + 16
GATHERED = COLUMNS_AT + 2 * COLUMNS


def gather_kernel(came_ref, query_ref, key_ref):
    planes = came_ref.shape[0]
    first = [came_ref[i, 0 : 2 * EACH, :].astype(jnp.float32) for i in range(planes)]
    second = [came_ref[i, 2 * EACH : 4 * EACH, :].astype(jnp.float32) for i in range(planes)]
    queries, keys = (
        jnp.concatenate([t[k * EACH : (k + 1) * EACH] for t in first], axis=0).astype(jnp.bfloat16)
        for k in range(2)
    )
    values = jnp.concatenate([t[0:EACH] for t in second], axis=0).astype(jnp.bfloat16)
    lane = lax.broadcasted_iota(jnp.int32, (EACH, LANES), 1)
    docs = jnp.zeros((EACH, LANES), jnp.float32)
    for i, tile in enumerate(second):
        docs = jnp.where(lane // EACH == i, pltpu.roll(tile[EACH:], EACH * i, 1), docs)
    docs = jnp.concatenate([docs, docs], axis=0).astype(jnp.bfloat16)
    query_ref[0:ROWS, :] = queries
    query_ref[ROWS : ROWS + 16, :] = docs
    for s in range(key_ref.shape[0]):
        key_ref[s, 0:ROWS, :] = (keys, values)[s % 2]
        key_ref[s, DOCS_AT:COLUMNS_AT, :] = docs
        for k in range(2):
            at = COLUMNS_AT + k * COLUMNS
            key_ref[s, at : at + COLUMNS, :] = came_ref[2 * (s % 8) + k, WEIGHT_AT:SENT, :]


def attend_kernel(
    place_ref, query_ref, key_ref, swapped_ref, out_ref, score_ref, keys_ref, values_ref
):
    z2, y, x, c = (place_ref[k] for k in range(4))

    @pl.when(c == 0)
    def _():
        keys_ref[...] = key_ref[:, 0:ROWS, :]
        values_ref[...] = swapped_ref[...]

    @pl.when(c != 0)
    def _():
        keys_ref[...] = swapped_ref[...]
        values_ref[...] = key_ref[:, 0:ROWS, :]

    stripe = 2 * BLOCK * 4

    def positions(z2, y, x, c, dim):
        index = lax.broadcasted_iota(jnp.int32, (ROWS, LANES), dim)
        first = (z2 * 4 + y) * BLOCK + EACH * (2 * x + c)
        return first + (index >> 3) * stripe + (index & 7)

    sources = key_ref.shape[0]
    key_docs = [
        key_ref[s, DOCS_AT:COLUMNS_AT, :].astype(jnp.float32)[0:1] for s in range(sources)
    ]
    key_pos = [positions(s // 8, y, s % 8 // 2, s % 2, 1)[0:1] for s in range(sources)]
    for first in range(0, query_ref.shape[0], 2):
        pair = (first, first + 1)
        queries = jnp.concatenate([query_ref[r, 0:ROWS, :] for r in pair], axis=0)
        query_docs = jnp.concatenate(
            [
                transposed(query_ref[r, ROWS : ROWS + 16, :].astype(jnp.float32)[0:1])
                for r in pair
            ],
            axis=0,
        )
        query_pos = jnp.concatenate([positions(z2, r, x, c, 0) for r in pair], axis=0)
        shape = query_pos.shape
        highest = jnp.full(shape, HIDDEN, jnp.float32)
        for s in range(sources):
            scores = lax.dot_general(
                queries,
                keys_ref[s],
                (((1,), (1,)), ((), ())),
                preferred_element_type=jnp.float32,
            )
            visible = (key_pos[s] <= query_pos) & (key_docs[s] == query_docs)
            scores = jnp.where(visible, scores, HIDDEN)
            score_ref[s] = scores
            highest = jnp.maximum(highest, scores)
        row_max = jnp.maximum(jnp.max(highest, axis=1, keepdims=True), LOWEST)
        row_max = jnp.broadcast_to(row_max, shape)
        total = jnp.zeros(shape, jnp.float32)
        mixed = jnp.zeros(shape, jnp.float32)
        for s in range(0, sources, 2):
            weights, values = [], []
            for k in (s, s + 1):
                weight = jnp.exp2((score_ref[k] - row_max) * FACTOR)
                total = total + weight
                weights.append(weight.astype(jnp.bfloat16))
                values.append(values_ref[k])
            mixed = mixed + jnp.dot(
                jnp.concatenate(weights, axis=1),
                jnp.concatenate(values, axis=0),
                preferred_element_type=jnp.float32,
            )
        row_sum = jnp.broadcast_to(jnp.sum(total, axis=1, keepdims=True), shape)
        means = jnp.where(row_sum > 0.0, mixed / row_sum, 0.0).astype(jnp.bfloat16)
        for k, r in enumerate(pair):
            rows = slice(k * ROWS, (k + 1) * ROWS)
            out_ref[r, 0:ROWS, :] = means[rows]
            stats = in_parts(row_max[rows].T[0:1]) + in_parts(row_sum[rows].T[0:1])
            stats = jnp.concatenate(stats + [jnp.zeros((10, LANES), jnp.float32)], axis=0)
            out_ref[r, ROWS : ROWS + 16, :] = stats.astype(jnp.bfloat16)


def columns_kernel(key_ref, after_ref, out_ref, half_ref):
    out_ref[...] = key_ref[:, COLUMNS_AT:GATHERED, :]
    half_ref[...] = key_ref[:, 0:ROWS, :]


def combine_kernel(part_ref, own_ref, other_ref, out_ref, same_own_ref, same_other_ref):
    same_own_ref[...] = own_ref[...]
    same_other_ref[...] = other_ref[...]
    parts = part_ref.shape[0]
    stats = [part_ref[r, ROWS : ROWS + 16, :].astype(jnp.float32) for r in range(parts)]
    maxima = [t[0:1] + t[1:2] + t[2:3] for t in stats]
    sums = [t[3:4] + t[4:5] + t[5:6] for t in stats]
    row_max = maxima[0]
    for m in maxima[1:]:
        row_max = jnp.maximum(row_max, m)
    scales = [jnp.exp2((m - row_max) * FACTOR) for m in maxima]
    scales = [scale * s for scale, s in zip(scales, sums)]
    row_sum = sum(scales)
    mixed = jnp.zeros((ROWS, HEAD_DIM), jnp.float32)
    for r in range(parts):
        mean = part_ref[r, 0:ROWS, :].astype(jnp.float32)
        mixed = mixed + mean * transposed(scales[r] / row_sum)
    out_ref[...] = mixed.astype(out_ref.dtype)


def product_kernel(place_ref, attended_ref, *refs):
    weights, (residual_ref, out_ref) = refs[:8], refs[8:]
    y, zp = place_ref[1], place_ref[4]
    groups = attended_ref.shape[0]
    total = jnp.zeros(out_ref.shape, jnp.float32)
    for p in range(groups):
        heads = [
            attended_ref[:, 2 * p + (zp ^ j)].astype(jnp.float32).reshape(BLOCK, HEAD_DIM)
            for j in range(2)
        ]
        left = jnp.concatenate(heads, axis=1).astype(jnp.bfloat16)
        blocks = []
        for k in range(2):
            rows = slice(k * COLUMNS, (k + 1) * COLUMNS)
            for z2 in range(2):
                for own, other in zip(weights[:4], weights[4:]):
                    halves = [w[z2 * groups + p, rows, :] for w in (own, other)]
                    blocks.append(jnp.concatenate(halves, axis=1))
        total = total + lax.dot_general(
            left,
            jnp.concatenate(blocks, axis=0),
            (((1,), (1,)), ((), ())),
            preferred_element_type=jnp.float32,
        )
    for zl in range(4):
        columns = slice(zl * LANES, (zl + 1) * LANES)
        summed = pltpu.roll(total[:, columns], y * COLUMNS, 1)
        out_ref[:, columns] = (residual_ref[:, columns].astype(jnp.float32) + summed).astype(
            out_ref.dtype
        )


def shards(query, key_states, value_states, doc_ids, out_weight, residual):
    groups = lax.axis_size(HEAD_AXES)
    planes = lax.axis_size(PLANES)
    spread = lax.axis_size(QUERY_AXES)
    sources = lax.axis_size(KEY_AXES)
    bf16, f32 = jnp.bfloat16, jnp.float32
    index = [lax.axis_index(a) for a in ("z2", "y", "x", "c", "zp")]
    place = jnp.stack(index)

    cut = [a.reshape(groups, EACH, -1) for a in (query, key_states, value_states)]
    by_rows = exchange(jnp.concatenate(cut, axis=1), HEAD_AXES)
    first = (2 * lax.axis_index("x") + lax.axis_index("c")) * EACH
    docs = jnp.roll(doc_ids, -first)
    docs = jnp.tile(docs.astype(bf16), 2 * LANES // BLOCK)
    extra = jnp.concatenate([out_weight.T, jnp.broadcast_to(docs, (16, 2 * LANES))])
    sent = call(
        send_kernel, jax.ShapeDtypeStruct((planes, SENT, LANES), bf16), [VMEM] * 2, "send"
    )(by_rows, extra)
    came = exchange(sent, PLANES)
    queries, keys = call(
        gather_kernel,
        [
            jax.ShapeDtypeStruct((ROWS + 16, LANES), bf16),
            jax.ShapeDtypeStruct((sources, GATHERED, LANES), bf16),
        ],
        [VMEM],
        "spread",
    )(came)
    keys = exchange(keys, KEY_AXES)
    queries = lax.all_gather(queries, QUERY_AXES)

    held = jax.ShapeDtypeStruct((sources, GATHERED - COLUMNS_AT, LANES), bf16)
    half = jax.ShapeDtypeStruct((sources, ROWS, LANES), bf16)
    own, half = call(
        columns_kernel, [held, half], [VMEM, pl.BlockSpec(memory_space=pl.ANY)], "columns"
    )(keys, queries)
    swapped = moved(half, lambda z, y, x, c: (z, y, x, 1 - c))

    parts = call(
        attend_kernel,
        jax.ShapeDtypeStruct((spread, ROWS + 16, LANES), bf16),
        [SMEM] + [VMEM] * 3,
        "attend",
        [
            pltpu.VMEM((sources, 2 * ROWS, LANES), f32),
            pltpu.VMEM((sources, ROWS, LANES), bf16),
            pltpu.VMEM((sources, ROWS, LANES), bf16),
        ],
        4 * spread * ROWS * sources * ROWS * HEAD_DIM,
        2 << 20,
    )(place, queries, keys, swapped)
    parts = exchange(parts, QUERY_AXES)

    def from_y(block, k):
        return moved(block, lambda z, y, x, c: (z, (y - k) % 4, x, c))

    other = moved(own, lambda z, y, x, c: (z ^ 2, y, x, c))
    last_own = from_y(own, 3)
    attended, own, other = call(
        combine_kernel,
        [jax.ShapeDtypeStruct((ROWS, HEAD_DIM), bf16), held, held],
        [VMEM] * 3,
        "combine",
    )(parts, own, other)
    weights = [own, from_y(own, 1), from_y(last_own, 3), last_own]
    weights += [other] + [from_y(other, k) for k in (1, 2, 3)]

    back = exchange(attended.reshape(planes, EACH, HEAD_DIM), PLANES)
    everyone = exchange(jnp.broadcast_to(back[None], (groups, *back.shape)), HEAD_AXES)
    return call(
        product_kernel,
        jax.ShapeDtypeStruct(residual.shape, residual.dtype),
        [SMEM] + [VMEM] * 10,
        "product",
        (),
        2 * BLOCK * 2048 * 512,
        3 << 20,
    )(place, everyone, *weights, residual)


def solution(mesh):
    names, sizes = zip(*AXES)
    fine = Mesh(mesh.devices.reshape(sizes), names)
    seq, head = SEQ_AXES, HEAD_AXES
    placed = (P(seq, head), P(seq, head), P(seq, head), P(seq), P(head, seq), P(seq, head))
    return jax.shard_map(
        shards, mesh=fine, in_specs=placed, out_specs=P(seq, head), check_vma=False
    )
```
